128 devices in a mesh: ctx: 8 (over z, core), head: 16 (over x, y).
Axes of the slice: x: 4, y: 4, z: 4, core: 2. Of those that a mesh axis runs over, the one named last changes fastest.
Arguments:
- values: bfloat16 [16384, 8192], P('ctx', 'head'), may hold values from -6 to 6
- step_sizes: float32 [16384, 128], P('ctx', 'head'), may hold values from 0.5 to 2
- decay_rates: float32 [128], P('head'), may hold values from 3.0517578e-05 to 0.1
- write_keys: bfloat16 [16384, 128], P('ctx'), may hold values from -0.5 to 0.5
- read_keys: bfloat16 [16384, 128], P('ctx'), may hold values from -0.5 to 0.5
- doc_ids: int32 [16384], P('ctx'), may hold values from 0 to 11, never falling along the last dimension, each value on 1 to 8192 neighbouring positions
- out_grad: bfloat16 [16384, 8192], P('ctx', 'head'), may hold values from -6 to 6
Outputs:
- value_grad: bfloat16 [16384, 8192], P('ctx', 'head')
- step_grad: float32 [16384, 128], P('ctx', 'head')
- write_grad: float32 [16384, 128], P(('ctx', 'head'))
- read_grad: float32 [16384, 128], P(('ctx', 'head'))
The draws below stay inside these ranges and needn't reach their ends.
Inputs may be any that keep to these rules, and one draw needn't show every extreme that they name: `doc_ids`: document numbers never fall along the row, start at 0, and each number forms one run of 1 to 8192 positions; one document has exactly 8192 positions.
All inputs are finite; a program needn't handle non-finite values.
Results may differ from the reference program's by a relative error of at most 0.001.
Values sent between devices are 32-bit elements; how exact they have to be, the bound alone decides.
A program may use at most 128 MiB of HBM per device.

```python
import math
from functools import partial
import jax
import jax.numpy as jnp
import numpy as np
from jax import lax

HEADS = 128
P_SIZE = 64
N = 128
QCHUNK = 256
DOCS = 12
TOKENS = 16384
LONGEST = 8192


def block_levels(stream_key, shape, cuts, low, top_value):
    def one(dim, blocks):
        heights = jax.random.uniform(jax.random.fold_in(jax.random.fold_in(stream_key, 6), dim), (blocks,), jnp.float32, low / len(cuts), top_value / len(cuts))
        return jnp.repeat(jnp.exp(heights), shape[dim] // blocks).reshape((-1,) + (1,) * (len(shape) - dim - 1))

    factor_of = one(*cuts[0])
    for cut in cuts[1:]:
        factor_of = factor_of * one(*cut)
    return factor_of


def profile(number_of, total, limit, slope):
    weights = [(1 << 20) // math.isqrt(grade ** slope) + 1 for grade in range(2, number_of + 1)]
    spare, given = total - limit - (number_of - 1), [1] * (number_of - 1)
    while spare > 0:
        free = [i for i in range(number_of - 1) if given[i] < limit]
        mass, budget = sum([weights[i] for i in free]), spare
        for i in free:
            more = min(limit - given[i], max(1, budget * weights[i] // mass), spare)
            given[i] = given[i] + more
            spare = spare - more
    return np.array([limit] + given)


def uneven_parts(rng, count, total, bound, lean):
    if count == 2:
        one = jax.random.randint(rng, (), max(1, total - bound), min(bound, total - 1) + 1)
        return jnp.stack([one, total - one])
    tallies = jnp.asarray(profile(count, total, bound, lean), jnp.int32)
    twos = (count - 1) // 2
    source_of, taker = tallies[1:1 + 2 * twos:2], tallies[2:2 + 2 * twos:2]
    room = jnp.minimum(source_of - 1, bound - taker)
    shifted = jax.random.randint(jax.random.fold_in(rng, 1), (twos,), 0, 1 << 20) % (room + 1)
    tallies = tallies.at[1:1 + 2 * twos:2].set(source_of - shifted).at[2:2 + 2 * twos:2].set(taker + shifted)
    return tallies[jax.random.permutation(jax.random.fold_in(rng, 2), count)]


def centred(stream_key, shape, deviation, limit, split=(), held_as=jnp.bfloat16):
    array = deviation * jax.random.normal(stream_key, shape, jnp.float32)
    if split:
        array = array * block_levels(stream_key, shape, split, -0.22, 0.18)
    return jnp.clip(array, -limit, limit).astype(held_as)


def setup_inputs(seed: int = 0) -> dict:
    key_list = jax.random.split(jax.random.key(seed), 8)
    values = centred(key_list[0], (TOKENS, HEADS * P_SIZE), 1.0, 6.0, ((0, 8), (1, 16)))
    step_sizes = jnp.clip(jnp.exp(math.log(2.0) - 1.3862944 * jax.random.uniform(key_list[1], (TOKENS, HEADS), jnp.float32) ** block_levels(key_list[1], (TOKENS, HEADS), ((0, 8), (1, 16)), -0.2, 0.2)), 0.5, 2.0)
    decay_rates = jnp.clip(jnp.exp(math.log(0.1) - 8.094623 * jax.random.uniform(key_list[2], (HEADS,), jnp.float32) ** block_levels(key_list[2], (HEADS,), ((0, 16),), -0.2, 0.2)), 3.0517578125e-05, 0.1)
    write_keys = centred(key_list[3], (TOKENS, N), N ** -0.5, 0.5, ((0, 8),))
    read_keys = centred(key_list[4], (TOKENS, N), N ** -0.5, 0.5, ((0, 8),))
    doc_ids = jnp.searchsorted(jnp.cumsum(uneven_parts(key_list[5], DOCS, TOKENS, LONGEST, 2)), jnp.arange(TOKENS), side="right").astype(jnp.int32)
    out_grad = centred(key_list[6], (TOKENS, HEADS * P_SIZE), 1.0, 6.0, ((0, 8), (1, 16)))
    return {"values": values, "step_sizes": step_sizes, "decay_rates": decay_rates, "write_keys": write_keys, "read_keys": read_keys, "doc_ids": doc_ids, "out_grad": out_grad}


def group_step(hidden_state, pieces, decay_rates):
    inputs, step_sizes, write_keys, read_keys, doc_starts = pieces
    highest = lax.Precision.HIGHEST
    length = inputs.shape[0]
    cumulative = jnp.cumsum(-step_sizes * decay_rates[None, :], axis=0).T
    doc_count = jnp.cumsum(doc_starts)
    rows = lax.broadcasted_iota(jnp.int32, (length, length), 0)
    cols = lax.broadcasted_iota(jnp.int32, (length, length), 1)
    same_doc = (doc_count[:, None] == doc_count[None, :]) & (rows >= cols)
    spread = jnp.where(same_doc[None], cumulative[:, :, None] - cumulative[:, None, :], 0.0)
    decays = jnp.where(same_doc[None], jnp.exp(spread), 0.0)
    scores = jnp.dot(read_keys, write_keys.T, precision=highest)
    weights = decays * scores[None] * step_sizes.T[:, None, :]
    output = jnp.einsum('hts,shp->thp', weights, inputs, precision=highest)
    reach = jnp.where((doc_count == 0)[None, :], jnp.exp(cumulative), 0.0)
    output = output + reach.T[:, :, None] * jnp.einsum('tn,hnp->thp', read_keys, hidden_state, precision=highest)
    to_end = decays[:, -1, :] * step_sizes.T
    next_state = jnp.einsum('sn,shp->hnp', write_keys, to_end.T[:, :, None] * inputs, precision=highest)
    next_state = next_state + reach[:, -1][:, None, None] * hidden_state
    return (next_state, output)

def span_forward(inputs, step_sizes, write_keys, read_keys, doc_starts, hidden_state, decay_rates, block_len):
    total = inputs.shape[0]
    blocks = total // block_len
    heads = inputs.shape[1]
    width = inputs.shape[2]
    states = write_keys.shape[1]
    pieces = (inputs.reshape(blocks, block_len, heads, width), step_sizes.reshape(blocks, block_len, heads), write_keys.reshape(blocks, block_len, states), read_keys.reshape(blocks, block_len, states), doc_starts.reshape(blocks, block_len))
    stepper = jax.checkpoint(partial(group_step, decay_rates=decay_rates))
    final, outputs = lax.scan(stepper, hidden_state, pieces)
    return (outputs.reshape(total, heads, width), final)

def reference(values, step_sizes, decay_rates, write_keys, read_keys, doc_ids, out_grad):
    inputs = values.astype(jnp.float32).reshape(TOKENS, HEADS, P_SIZE)
    doc_starts = jnp.concatenate([jnp.ones((1,), jnp.float32), (doc_ids[1:] != doc_ids[:-1]).astype(jnp.float32)])
    empty = jnp.zeros((HEADS, N, P_SIZE), jnp.float32)

    def forward(inputs_in, steps_in, writes_in, reads_in):
        output, final = span_forward(inputs_in, steps_in, writes_in, reads_in, doc_starts, empty, decay_rates, QCHUNK)
        return output
    output, pullback = jax.vjp(forward, inputs, step_sizes, write_keys.astype(jnp.float32), read_keys.astype(jnp.float32))
    grads = pullback(out_grad.astype(jnp.float32).reshape(TOKENS, HEADS, P_SIZE))
    value_grad = grads[0].reshape(TOKENS, HEADS * P_SIZE).astype(jnp.bfloat16)
    return (value_grad, grads[1], grads[2], grads[3])
```

```python
from functools import partial

import jax
import jax.numpy as jnp
from jax import lax
from jax.experimental import pallas as pl
from jax.experimental.pallas import tpu as pltpu
from jax.sharding import PartitionSpec as P

QCHUNK = 256
ROUNDS = 3
F32 = jnp.float32
BF16 = jnp.bfloat16


def two_parts(value):
    high = value.astype(BF16)
    return high, (value - high.astype(F32)).astype(BF16)


def three_parts(value):
    high = value.astype(BF16)
    rest = value - high.astype(F32)
    middle = rest.astype(BF16)
    return high, middle, (rest - middle.astype(F32)).astype(BF16)


def dot(left, right, contract):
    return lax.dot_general(left, right, ((contract[:1], contract[1:]), ((), ())), preferred_element_type=F32)


def dot_nn(left, right):
    return dot(left, right, (1, 0))


def dot_nt(left, right):
    return dot(left, right, (1, 1))


def dot_tn(left, right):
    return dot(left, right, (0, 0))


def mod(value, count):
    return lax.rem(value + count, count)


def kernel(
    n_ctx, n_head, x_ref, g_ref, step_ref, rate_ref, w_ref, r_ref, doc_ref,
    vg_ref, sg_ref, wg_ref, rg_ref,
    xhi, xlo, ghi, glo, scale, out_acc, val_acc, doc_col, rw, rw_in,
    state, back, half, phi_f, phi_b, sphi, splo, bphi, bplo,
    f_send, f_recv, b_send, b_recv, ctx_ss, ctx_rs, rw_ss, rw_rs,
):
    length, width = x_ref.shape
    heads = step_ref.shape[0]
    head_size = width // heads
    states = w_ref.shape[1]
    q = QCHUNK
    chunks = length // q
    block = length // n_head
    per = q // block
    lanes = 128
    doc_rows = q // lanes
    me_ctx, me = lax.axis_index("ctx"), lax.axis_index("head")

    barrier = pltpu.get_barrier_semaphore()
    for step in (1, 2):
        for side in (step, n_ctx - step):
            pl.semaphore_signal(barrier, inc=1, device_id={"ctx": mod(me_ctx + side, n_ctx)})

    @pl.loop(1, n_head)
    def _(o):
        pl.semaphore_signal(barrier, inc=1, device_id={"head": mod(me + o, n_head)})

    head_rows = lax.broadcasted_iota(jnp.int32, (heads, width), 0)
    head_lanes = lax.broadcasted_iota(jnp.int32, (heads, width), 1)
    of_head = jnp.where(head_lanes // head_size == head_rows, 1.0, 0.0)
    of_head16 = of_head.astype(BF16)
    spread3 = jnp.concatenate([of_head] * 3, axis=0).astype(BF16)
    square_rows = lax.broadcasted_iota(jnp.int32, (q, q), 0)
    square_cols = lax.broadcasted_iota(jnp.int32, (q, q), 1)
    rate = jnp.zeros((heads, 1), F32)
    rate_row = lax.broadcasted_iota(jnp.int32, (heads, 1), 0)
    for h in range(heads):
        rate = jnp.where(rate_row == h, rate_ref[h], rate)

    def rows_of(c):
        return pl.ds(pl.multiple_of(c * q, q), q)

    def doc_row(c):
        return jnp.concatenate(
            [doc_ref[pl.ds(c * doc_rows + k, 1), :] for k in range(doc_rows)], axis=1
        ).astype(F32)

    def first_doc(c):
        return doc_ref[pl.ds(c * doc_rows, 1), 0:1].astype(F32)

    def last_doc(c):
        return doc_ref[pl.ds(c * doc_rows + doc_rows - 1, 1), lanes - 1:lanes].astype(F32)

    def to_lanes(column):
        return jnp.sum(of_head * column, axis=0, keepdims=True)

    def widen(value):
        parts = jnp.concatenate([p.astype(F32) for p in three_parts(value)], axis=0)
        return dot_tn(parts.astype(BF16), spread3)

    def stacked_dot(value, right):
        parts = jnp.concatenate([p.astype(F32) for p in three_parts(value)], axis=0)
        made = dot_nn(parts.astype(BF16), right)
        return made[:heads] + made[heads:2 * heads] + made[2 * heads:]

    state[0] = jnp.zeros((states, width), F32)
    back[chunks] = jnp.zeros((states, width), F32)

    def local_states(c, total):
        rows = rows_of(c)
        steps = step_ref[:, rows]
        upper = (square_rows <= square_cols).astype(F32).astype(BF16)
        decay = stacked_dot(-steps * rate, upper)
        whole = decay[:, q - 1:q]
        middle = 0.5 * whole
        g_scaled = g_ref[rows, :].astype(F32) * widen(jnp.exp(decay - middle))
        high, low = two_parts(g_scaled)
        ghi[rows, :], glo[rows, :] = high, low
        x_scale = widen(jnp.exp(middle - decay) * steps)
        scale[rows, :] = x_scale
        xh, xl = two_parts(x_ref[rows, :].astype(F32) * x_scale)
        xhi[rows, :], xlo[rows, :] = xh, xl
        docs = doc_row(c)
        column = jnp.transpose(jnp.broadcast_to(docs, (lanes, q)))
        doc_col[rows, :] = column
        half_row = to_lanes(jnp.exp(middle))
        half[pl.ds(c, 1), :] = half_row
        w_last = jnp.where(column == docs[:, q - 1:], w_ref[rows, :].astype(F32), 0.0).astype(BF16)
        r_first = jnp.where(column == docs[:, :1], r_ref[rows, :].astype(F32), 0.0).astype(BF16)
        made = (dot_tn(w_last, xh) + dot_tn(w_last, xl)) * half_row
        before = last_doc(jnp.maximum(c - 1, 0))
        kept = jnp.where(before == docs[:, q - 1:], half_row * half_row, 0.0)
        state[c + 1] = made + kept * state[c]
        back[c] = (dot_tn(r_first, high) + dot_tn(r_first, low)) * half_row
        phi_f[pl.ds(c, 1), :] = to_lanes(jnp.exp(total))
        return total + whole

    total = lax.fori_loop(0, chunks, local_states, jnp.zeros((heads, 1), F32))
    phi_f[pl.ds(chunks, 1), :] = to_lanes(jnp.exp(total))
    phi_b[pl.ds(chunks, 1), :] = jnp.ones((1, width), F32)

    @pl.loop(0, chunks)
    def _(i):
        c = chunks - 1 - i
        half_row = half[pl.ds(c, 1), :]
        square = half_row * half_row
        kept = jnp.where(first_doc(jnp.minimum(c + 1, chunks - 1)) == first_doc(c), square, 0.0)
        back[c] = back[c] + kept * back[c + 1]
        phi_b[pl.ds(c, 1), :] = phi_b[pl.ds(c + 1, 1), :] * square

    whole_row = to_lanes(total)
    first_here, last_here = first_doc(0), last_doc(chunks - 1)

    def put(ref, which, value, span, doc):
        ref[which, 0:states, :] = value
        ref[which, states:states + 1, :] = span
        ref[which, states + 1:states + 2, :] = jnp.broadcast_to(doc, (1, width))

    def span_of(ref, which):
        return ref[which, states:states + 1, :]

    def doc_of(ref, which):
        return ref[which, states + 1:states + 2, :]

    def value_of(ref, which):
        return ref[which, 0:states, :]

    def ctx_copies(which, step):
        made = []
        for side, send, recv, k in ((step, f_send, f_recv, 0), (n_ctx - step, b_send, b_recv, 1)):
            made.append(
                pltpu.make_async_remote_copy(
                    src_ref=send.at[which], dst_ref=recv.at[which],
                    send_sem=ctx_ss.at[which, k], recv_sem=ctx_rs.at[which, k],
                    device_id={"ctx": mod(me_ctx + side, n_ctx)},
                )
            )
        return made

    def intra(c):
        rows = rows_of(c)
        reads, writes = r_ref[rows, :], w_ref[rows, :]
        column = doc_col[rows, :]
        same = jnp.concatenate([column] * doc_rows, axis=1) == doc_row(c)
        lower = same & (square_rows >= square_cols)
        upper = same & (square_rows <= square_cols)
        xh, xl, gh, gl = xhi[rows, :], xlo[rows, :], ghi[rows, :], glo[rows, :]
        high, low = two_parts(jnp.where(lower, dot_nt(reads, writes), 0.0))
        out_acc[rows, :] = dot_nn(high, xh) + dot_nn(high, xl) + dot_nn(low, xh)
        high, low = two_parts(jnp.where(upper, dot_nt(writes, reads), 0.0))
        val_acc[rows, :] = dot_nn(high, gh) + dot_nn(high, gl) + dot_nn(low, gh)
        pairs = dot_nt(gh, xh) + dot_nt(gh, xl) + dot_nt(gl, xh)
        high, low = two_parts(jnp.where(lower, pairs, 0.0))
        to_read = dot_nn(high, writes) + dot_nn(low, writes)
        to_write = dot_tn(high, reads) + dot_tn(low, reads)
        for j in range(per):
            rw[c * per + j, 0] = to_write[j * block:(j + 1) * block]
            rw[c * per + j, 1] = to_read[j * block:(j + 1) * block]

    put(f_send, 0, state[chunks], whole_row, last_here)
    put(b_send, 0, back[0], whole_row, first_here)
    pl.semaphore_wait(barrier, n_head - 1 + 4)
    first_copies = ctx_copies(0, 1)
    for copy in first_copies:
        copy.start()
    cut = (0, (3 * chunks) // 8, (6 * chunks) // 8, chunks)
    pl.loop(cut[0], cut[1])(intra)
    for copy in first_copies:
        copy.wait()
    whole_decay = jnp.exp(whole_row)
    put(
        f_send, 1,
        value_of(f_send, 0) + jnp.where(doc_of(f_recv, 0) == last_here, whole_decay, 0.0) * value_of(f_recv, 0),
        whole_row + span_of(f_recv, 0), last_here,
    )
    put(
        b_send, 1,
        value_of(b_send, 0) + jnp.where(doc_of(b_recv, 0) == first_here, whole_decay, 0.0) * value_of(b_recv, 0),
        whole_row + span_of(b_recv, 0), first_here,
    )
    second_copies = ctx_copies(1, 2)
    for copy in second_copies:
        copy.start()
    pl.loop(cut[1], cut[2])(intra)
    for copy in second_copies:
        copy.wait()
    for send, recv, doc in ((f_send, f_recv, last_here), (b_send, b_recv, first_here)):
        joined = jnp.where(doc_of(recv, 1) == doc, jnp.exp(span_of(send, 1)), 0.0)
        put(send, 2, value_of(send, 1) + joined * value_of(recv, 1), whole_row, doc)
    third_copies = ctx_copies(2, 1)
    for copy in third_copies:
        copy.start()
    pl.loop(cut[2], cut[3])(intra)
    for copy in third_copies:
        copy.wait()

    doc_before, doc_after = doc_of(f_recv, 2)[:, :1], doc_of(b_recv, 2)[:, :1]

    def previous_doc(c):
        return jnp.where(c == 0, doc_before, last_doc(jnp.maximum(c - 1, 0)))

    def next_doc(c):
        return jnp.where(c == chunks - 1, doc_after, first_doc(jnp.minimum(c + 1, chunks - 1)))

    def state_at(k, doc):
        return state[k] + jnp.where(doc == doc_before, phi_f[pl.ds(k, 1), :], 0.0) * value_of(f_recv, 2)

    def back_at(k, doc):
        return back[k] + jnp.where(doc == doc_after, phi_b[pl.ds(k, 1), :], 0.0) * value_of(b_recv, 2)

    def rw_copy(b):
        o = mod(b - me, n_head)
        return pltpu.make_async_remote_copy(
            src_ref=rw.at[b], dst_ref=rw_in.at[o], send_sem=rw_ss.at[o], recv_sem=rw_rs.at[o],
            device_id={"head": b},
        )

    @pl.loop(0, chunks)
    def _(i):
        c = lax.rem(me // per + 1 + i, chunks)
        rows = rows_of(c)
        column = doc_col[rows, :]
        half_row = half[pl.ds(c, 1), :]
        before, after = previous_doc(c), next_doc(c)
        sh, sl = two_parts(state_at(c, before) * half_row)
        sphi[c], splo[c] = sh, sl
        bh, bl = two_parts(back_at(c + 1, after) * half_row)
        bphi[c], bplo[c] = bh, bl
        to_read = dot_nt(ghi[rows, :], sh) + dot_nt(ghi[rows, :], sl) + dot_nt(glo[rows, :], sh)
        to_write = dot_nt(xhi[rows, :], bh) + dot_nt(xhi[rows, :], bl) + dot_nt(xlo[rows, :], bh)
        to_read = jnp.where(column == before, to_read, 0.0)
        to_write = jnp.where(column == after, to_write, 0.0)
        for j in range(per):
            b = c * per + j
            rw[b, 0] += to_write[j * block:(j + 1) * block]
            rw[b, 1] += to_read[j * block:(j + 1) * block]

            @pl.when(b != me)
            def _():
                rw_copy(b).start()

    @pl.loop(0, chunks)
    def _(c):
        rows = rows_of(c)
        column = doc_col[rows, :]
        docs = doc_row(c)
        before, after, last = previous_doc(c), next_doc(c), docs[:, q - 1:]
        reads = jnp.where(column == before, r_ref[rows, :].astype(F32), 0.0).astype(BF16)
        writes = jnp.where(column == after, w_ref[rows, :].astype(F32), 0.0).astype(BF16)
        out = out_acc[rows, :] + dot_nn(reads, sphi[c]) + dot_nn(reads, splo[c])
        val = val_acc[rows, :] + dot_nn(writes, bphi[c]) + dot_nn(writes, bplo[c])
        vg_ref[rows, :] = (scale[rows, :] * val).astype(BF16)
        g_scaled = ghi[rows, :].astype(F32) + glo[rows, :].astype(F32)
        x_scaled = xhi[rows, :].astype(F32) + xlo[rows, :].astype(F32)
        high, low = two_parts(x_scaled * val)
        at_write = dot_nt(of_head16, high) + dot_nt(of_head16, low)
        high, low = two_parts(g_scaled * out)
        at_read = dot_nt(of_head16, high) + dot_nt(of_head16, low)
        lower = (jnp.concatenate([column] * doc_rows, axis=1) == docs) & (square_rows >= square_cols)
        later = stacked_dot(at_read - at_write, lower.astype(F32).astype(BF16))
        crossing = jnp.sum(state_at(c + 1, last) * back_at(c + 1, after), axis=0, keepdims=True)
        crossing = jnp.sum(of_head * crossing, axis=1, keepdims=True)
        crossing = jnp.where(last == after, crossing, 0.0)
        later = later + jnp.where(docs == last, crossing, 0.0)
        sg_ref[:, rows] = at_write / step_ref[:, rows] - rate * later

    @pl.loop(1, n_head)
    def _(o):
        rw_copy(mod(me + o, n_head)).wait_recv()

    def gathered(k):
        return lax.fori_loop(1, n_head, lambda o, held: held + rw_in[o, k], rw[me, k])

    wg_ref[...] = gathered(0)
    rg_ref[...] = gathered(1)

    @pl.loop(1, n_head)
    def _(o):
        rw_copy(mod(me + o, n_head)).wait_send()


def shards(mesh_shape, values, step_sizes, decay_rates, write_keys, read_keys, doc_ids, out_grad):
    n_ctx, n_head = mesh_shape
    length, width = values.shape
    heads = decay_rates.shape[0]
    states = write_keys.shape[1]
    chunks = length // QCHUNK
    block = length // n_head
    vmem = pl.BlockSpec(memory_space=pltpu.VMEM)
    wide16 = pltpu.VMEM((length, width), BF16)
    wide32 = pltpu.VMEM((length, width), F32)
    message = pltpu.VMEM((ROUNDS, states + 8, width), F32)
    value_grad, step_grad, write_grad, read_grad = pl.pallas_call(
        partial(kernel, n_ctx, n_head),
        out_shape=(
            jax.ShapeDtypeStruct((length, width), BF16),
            jax.ShapeDtypeStruct((heads, length), F32),
            jax.ShapeDtypeStruct((block, states), F32),
            jax.ShapeDtypeStruct((block, states), F32),
        ),
        in_specs=[vmem, vmem, vmem, pl.BlockSpec(memory_space=pltpu.SMEM), vmem, vmem, vmem],
        out_specs=(vmem, vmem, vmem, vmem),
        scratch_shapes=[
            wide16, wide16, wide16, wide16, wide32, wide32, wide32,
            pltpu.VMEM((length, 128), F32),
            pltpu.VMEM((n_head, 2, block, states), F32),
            pltpu.VMEM((n_head, 2, block, states), F32),
            pltpu.VMEM((chunks + 1, states, width), F32),
            pltpu.VMEM((chunks + 1, states, width), F32),
            pltpu.VMEM((chunks, width), F32),
            pltpu.VMEM((chunks + 1, width), F32),
            pltpu.VMEM((chunks + 1, width), F32),
            pltpu.VMEM((chunks, states, width), BF16),
            pltpu.VMEM((chunks, states, width), BF16),
            pltpu.VMEM((chunks, states, width), BF16),
            pltpu.VMEM((chunks, states, width), BF16),
            message, message, message, message,
            pltpu.SemaphoreType.DMA((ROUNDS, 2)),
            pltpu.SemaphoreType.DMA((ROUNDS, 2)),
            pltpu.SemaphoreType.DMA((n_head,)),
            pltpu.SemaphoreType.DMA((n_head,)),
        ],
        compiler_params=pltpu.CompilerParams(
            collective_id=0, has_side_effects=True, vmem_limit_bytes=60 * 2**20
        ),
    )(
        values, out_grad, step_sizes.T, decay_rates, write_keys, read_keys,
        doc_ids.reshape(length // 128, 128),
    )
    return value_grad, step_grad.T, write_grad, read_grad


def solution(mesh):
    return jax.shard_map(
        partial(shards, (mesh.shape["ctx"], mesh.shape["head"])),
        mesh=mesh,
        in_specs=(
            P("ctx", "head"),
            P("ctx", "head"),
            P("head"),
            P("ctx", None),
            P("ctx", None),
            P("ctx"),
            P("ctx", "head"),
        ),
        out_specs=(
            P("ctx", "head"),
            P("ctx", "head"),
            P(("ctx", "head"), None),
            P(("ctx", "head"), None),
        ),
        check_vma=False,
    )
```

```python
import math
from functools import partial

import jax
import jax.numpy as jnp
from jax import lax
from jax.experimental import pallas as pl
from jax.experimental.pallas import tpu as pltpu
from jax.sharding import PartitionSpec as P

QCHUNK = 256
F32 = jnp.float32
BF16 = jnp.bfloat16


def two_parts(value):
    high = value.astype(BF16)
    return high, (value - high.astype(F32)).astype(BF16)


def three_parts(value):
    high = value.astype(BF16)
    rest = value - high.astype(F32)
    middle = rest.astype(BF16)
    return high, middle, (rest - middle.astype(F32)).astype(BF16)


def dot(left, right, contract):
    return lax.dot_general(left, right, ((contract[:1], contract[1:]), ((), ())), preferred_element_type=F32)


def dot_nn(left, right):
    return dot(left, right, (1, 0))


def dot_nt(left, right):
    return dot(left, right, (1, 1))


def dot_tn(left, right):
    return dot(left, right, (0, 0))


def mod(value, count):
    return lax.rem(value + count, count)


def kernel(
    n_ctx, n_head, x_ref, g_ref, step_ref, rate_ref, w_ref, r_ref, doc_ref,
    vg_ref, sg_ref, wg_ref, rg_ref,
    xhi, xlo, ghi, glo, scale, out_acc, val_acc, doc_col,
    r_acc, w_acc, r_in, w_in, r_in2, w_in2,
    state, back, half, phi_f, phi_b, sphi, splo, bphi, bplo,
    e_out, b_out, e_sib, b_sib, f_out, k_out, f_in, k_in, s_out, g_out, s_in, g_in,
    sib_ss, sib_rs, z_ss, z_rs, last_ss, last_rs,
    r_ss, r_rs, w_ss, w_rs, r2_ss, r2_rs, w2_ss, w2_rs,
):
    length, width = x_ref.shape
    heads = step_ref.shape[0]
    head_size = width // heads
    states = w_ref.shape[1]
    q = QCHUNK
    chunks = length // q
    side = math.isqrt(n_head)
    n_z = n_ctx // 2
    group = length // side
    block = length // n_head
    lanes = 128
    doc_rows = q // lanes
    hw = width // 2
    me_ctx, me = lax.axis_index("ctx"), lax.axis_index("head")
    me_z, core = me_ctx // 2, lax.rem(me_ctx, 2)
    me_x, me_y = me // side, lax.rem(me, side)

    def at_z(z):
        return {"ctx": z * 2 + core}

    def at_xy(x, y):
        return {"head": x * side + y}

    sibling = {"ctx": me_ctx + 1 - 2 * core}

    def put(ref, which, value, span, doc):
        ref[which, 0:states, :] = value
        ref[which, states:states + 1, :] = span
        ref[which, states + 1:states + 2, :] = jnp.broadcast_to(doc, (1, hw))

    for far in range(2):
        for ref in (f_in, k_in):
            put(ref, far, jnp.zeros((states, hw), F32), jnp.zeros((1, hw), F32), jnp.full((1, 1), -1.0, F32))

    barrier = pltpu.get_barrier_semaphore()
    pl.semaphore_signal(barrier, inc=1, device_id=sibling)
    for o in range(1, n_z):
        pl.semaphore_signal(barrier, inc=1, device_id=at_z(mod(me_z + o, n_z)))
    for o in range(1, side):
        pl.semaphore_signal(barrier, inc=1, device_id=at_xy(mod(me_x + o, side), me_y))
        pl.semaphore_signal(barrier, inc=1, device_id=at_xy(me_x, mod(me_y + o, side)))

    head_rows = lax.broadcasted_iota(jnp.int32, (heads, width), 0)
    head_lanes = lax.broadcasted_iota(jnp.int32, (heads, width), 1)
    of_head = jnp.where(head_lanes // head_size == head_rows, 1.0, 0.0)
    of_head16 = of_head.astype(BF16)
    spread3 = jnp.concatenate([of_head] * 3, axis=0).astype(BF16)
    square_rows = lax.broadcasted_iota(jnp.int32, (q, q), 0)
    square_cols = lax.broadcasted_iota(jnp.int32, (q, q), 1)
    rate = jnp.zeros((heads, 1), F32)
    rate_row = lax.broadcasted_iota(jnp.int32, (heads, 1), 0)
    for h in range(heads):
        rate = jnp.where(rate_row == h, rate_ref[h], rate)

    def rows_of(c):
        return pl.ds(pl.multiple_of(c * q, q), q)

    def doc_row(c):
        return jnp.concatenate(
            [doc_ref[pl.ds(c * doc_rows + k, 1), :] for k in range(doc_rows)], axis=1
        ).astype(F32)

    def first_doc(c):
        return doc_ref[pl.ds(c * doc_rows, 1), 0:1].astype(F32)

    def last_doc(c):
        return doc_ref[pl.ds(c * doc_rows + doc_rows - 1, 1), lanes - 1:lanes].astype(F32)

    def to_lanes(column):
        return jnp.sum(of_head * column, axis=0, keepdims=True)

    def widen(value):
        parts = jnp.concatenate([p.astype(F32) for p in three_parts(value)], axis=0)
        return dot_tn(parts.astype(BF16), spread3)

    def stacked_dot(value, right):
        parts = jnp.concatenate([p.astype(F32) for p in three_parts(value)], axis=0)
        made = dot_nn(parts.astype(BF16), right)
        return made[:heads] + made[heads:2 * heads] + made[2 * heads:]

    state[0] = jnp.zeros((states, width), F32)
    back[chunks] = jnp.zeros((states, width), F32)

    def local_states(c, total):
        rows = rows_of(c)
        steps = step_ref[:, rows]
        upper = (square_rows <= square_cols).astype(F32).astype(BF16)
        decay = stacked_dot(-steps * rate, upper)
        whole = decay[:, q - 1:q]
        middle = 0.5 * whole
        g_scaled = g_ref[rows, :].astype(F32) * widen(jnp.exp(decay - middle))
        high, low = two_parts(g_scaled)
        ghi[rows, :], glo[rows, :] = high, low
        x_scale = widen(jnp.exp(middle - decay) * steps)
        scale[rows, :] = x_scale
        xh, xl = two_parts(x_ref[rows, :].astype(F32) * x_scale)
        xhi[rows, :], xlo[rows, :] = xh, xl
        docs = doc_row(c)
        column = jnp.transpose(jnp.broadcast_to(docs, (lanes, q)))
        doc_col[rows, :] = column
        half_row = to_lanes(jnp.exp(middle))
        half[pl.ds(c, 1), :] = half_row
        w_last = jnp.where(column == docs[:, q - 1:], w_ref[rows, :].astype(F32), 0.0).astype(BF16)
        r_first = jnp.where(column == docs[:, :1], r_ref[rows, :].astype(F32), 0.0).astype(BF16)
        made = (dot_tn(w_last, xh) + dot_tn(w_last, xl)) * half_row
        before = last_doc(jnp.maximum(c - 1, 0))
        kept = jnp.where(before == docs[:, q - 1:], half_row * half_row, 0.0)
        state[c + 1] = made + kept * state[c]
        back[c] = (dot_tn(r_first, high) + dot_tn(r_first, low)) * half_row
        phi_f[pl.ds(c, 1), :] = to_lanes(jnp.exp(total))
        return total + whole

    total = lax.fori_loop(0, chunks, local_states, jnp.zeros((heads, 1), F32))
    phi_f[pl.ds(chunks, 1), :] = to_lanes(jnp.exp(total))
    phi_b[pl.ds(chunks, 1), :] = jnp.ones((1, width), F32)

    @pl.loop(0, chunks)
    def _(i):
        c = chunks - 1 - i
        half_row = half[pl.ds(c, 1), :]
        square = half_row * half_row
        kept = jnp.where(first_doc(jnp.minimum(c + 1, chunks - 1)) == first_doc(c), square, 0.0)
        back[c] = back[c] + kept * back[c + 1]
        phi_b[pl.ds(c, 1), :] = phi_b[pl.ds(c + 1, 1), :] * square

    whole_row = to_lanes(total)
    first_here, last_here = first_doc(0), last_doc(chunks - 1)

    def span_of(ref, which):
        return ref[which, states:states + 1, :]

    def doc_of(ref, which):
        return ref[which, states + 1:states + 2, :]

    def value_of(ref, which):
        return ref[which, 0:states, :]

    def joined(near, near_doc, near_span, far, far_doc):
        return near + jnp.where(near_doc == far_doc, jnp.exp(near_span), 0.0) * far

    def sib_copy(k, src, dst, ss, rs):
        return pltpu.make_async_remote_copy(
            src_ref=src, dst_ref=dst, send_sem=ss.at[k], recv_sem=rs.at[k], device_id=sibling
        )

    def z_copy(k, far):
        src, dst, to = (f_out, f_in, me_z + far) if k == 0 else (k_out, k_in, me_z - far)
        return pltpu.make_async_remote_copy(
            src_ref=src.at[0], dst_ref=dst.at[far - 1], send_sem=z_ss.at[k, far - 1],
            recv_sem=z_rs.at[k, far - 1], device_id=at_z(to),
        )

    def intra(c):
        rows = rows_of(c)
        reads, writes = r_ref[rows, :], w_ref[rows, :]
        column = doc_col[rows, :]
        same = jnp.concatenate([column] * doc_rows, axis=1) == doc_row(c)
        lower = same & (square_rows >= square_cols)
        upper = same & (square_rows <= square_cols)
        xh, xl, gh, gl = xhi[rows, :], xlo[rows, :], ghi[rows, :], glo[rows, :]
        high, low = two_parts(jnp.where(lower, dot_nt(reads, writes), 0.0))
        out_acc[rows, :] = dot_nn(high, xh) + dot_nn(high, xl) + dot_nn(low, xh)
        high, low = two_parts(jnp.where(upper, dot_nt(writes, reads), 0.0))
        val_acc[rows, :] = dot_nn(high, gh) + dot_nn(high, gl) + dot_nn(low, gh)
        pairs = dot_nt(gh, xh) + dot_nt(gh, xl) + dot_nt(gl, xh)
        high, low = two_parts(jnp.where(lower, pairs, 0.0))
        to_read = dot_nn(high, writes) + dot_nn(low, writes)
        to_write = dot_tn(high, reads) + dot_tn(low, reads)
        r_acc[rows, :] = to_read
        w_acc[rows, :] = to_write

    for k in range(2):
        lane = slice(k * hw, (k + 1) * hw)
        put(e_out, k, state[chunks][:, lane], whole_row[:, lane], last_here)
        put(b_out, k, back[0][:, lane], whole_row[:, lane], first_here)
    pl.semaphore_wait(barrier, 1 + n_z - 1 + 2 * (side - 1))
    sib_copies = (
        sib_copy(0, e_out.at[1 - core], e_sib.at[0], sib_ss, sib_rs),
        sib_copy(1, b_out.at[1 - core], b_sib.at[0], sib_ss, sib_rs),
    )
    for copy in sib_copies:
        copy.start()
    cuts = (0, chunks // 8, (7 * chunks) // 8, chunks)
    pl.loop(cuts[0], cuts[1])(intra)
    for copy in sib_copies:
        copy.wait()
    low, mine, other = core == 0, core, 0
    e_low = jnp.where(low, value_of(e_out, mine), value_of(e_sib, other))
    e_high = jnp.where(low, value_of(e_sib, other), value_of(e_out, mine))
    b_low = jnp.where(low, value_of(b_out, mine), value_of(b_sib, other))
    b_high = jnp.where(low, value_of(b_sib, other), value_of(b_out, mine))
    span_low = jnp.where(low, span_of(e_out, mine), span_of(e_sib, other))
    span_high = jnp.where(low, span_of(e_sib, other), span_of(e_out, mine))
    last_low = jnp.where(low, doc_of(e_out, mine), doc_of(e_sib, other))
    last_high = jnp.where(low, doc_of(e_sib, other), doc_of(e_out, mine))
    first_low = jnp.where(low, doc_of(b_out, mine), doc_of(b_sib, other))
    first_high = jnp.where(low, doc_of(b_sib, other), doc_of(b_out, mine))
    put(f_out, 0, joined(e_high, last_high, span_high, e_low, last_low), span_low + span_high, last_high)
    put(k_out, 0, joined(b_low, first_low, span_low, b_high, first_high), span_low + span_high, first_low)
    for far in (1, 2):
        if far < n_z:

            @pl.when(me_z + far < n_z)
            def _():
                z_copy(0, far).start()

            @pl.when(me_z - far >= 0)
            def _():
                z_copy(1, far).start()

    pl.loop(cuts[1], cuts[2], unroll=2)(intra)
    for far in (1, 2):
        if far < n_z:

            @pl.when(me_z - far >= 0)
            def _():
                z_copy(0, far).wait_recv()

            @pl.when(me_z + far < n_z)
            def _():
                z_copy(1, far).wait_recv()

    s_chip = joined(value_of(f_in, 0), doc_of(f_in, 0), span_of(f_in, 0), value_of(f_in, 1), doc_of(f_in, 1))
    g_chip = joined(value_of(k_in, 0), doc_of(k_in, 0), span_of(k_in, 0), value_of(k_in, 1), doc_of(k_in, 1))
    s_high = joined(value_of(e_out, mine), last_low, span_low, s_chip, doc_of(f_in, 0))
    s_high = jnp.where(low, s_high, joined(value_of(e_sib, other), last_low, span_low, s_chip, doc_of(f_in, 0)))
    g_low = joined(value_of(b_sib, other), first_high, span_high, g_chip, doc_of(k_in, 0))
    g_low = jnp.where(low, g_low, joined(value_of(b_out, mine), first_high, span_high, g_chip, doc_of(k_in, 0)))
    s_doc_low, s_doc_high = doc_of(f_in, 0), last_low
    g_doc_low, g_doc_high = first_high, doc_of(k_in, 0)
    put(s_out, 0, jnp.where(low, s_high, s_chip), span_low, jnp.where(low, s_doc_high, s_doc_low))
    put(g_out, 0, jnp.where(low, g_chip, g_low), span_low, jnp.where(low, g_doc_high, g_doc_low))
    last_copies = (
        sib_copy(0, s_out.at[0], s_in.at[mine], last_ss, last_rs),
        sib_copy(1, g_out.at[0], g_in.at[mine], last_ss, last_rs),
    )
    for copy in last_copies:
        copy.start()
    put(s_in, mine, jnp.where(low, s_chip, s_high), span_low, jnp.where(low, s_doc_low, s_doc_high))
    put(g_in, mine, jnp.where(low, g_low, g_chip), span_low, jnp.where(low, g_doc_low, g_doc_high))
    pl.loop(cuts[2], cuts[3])(intra)
    for copy in last_copies:
        copy.wait()

    doc_before, doc_after = doc_of(s_in, 0)[:, :1], doc_of(g_in, 0)[:, :1]

    def previous_doc(c):
        return jnp.where(c == 0, doc_before, last_doc(jnp.maximum(c - 1, 0)))

    def next_doc(c):
        return jnp.where(c == chunks - 1, doc_after, first_doc(jnp.minimum(c + 1, chunks - 1)))

    def state_at(k, doc):
        entered = jnp.concatenate([value_of(s_in, 0), value_of(s_in, 1)], axis=1)
        return state[k] + jnp.where(doc == doc_before, phi_f[pl.ds(k, 1), :], 0.0) * entered

    def back_at(k, doc):
        entered = jnp.concatenate([value_of(g_in, 0), value_of(g_in, 1)], axis=1)
        return back[k] + jnp.where(doc == doc_after, phi_b[pl.ds(k, 1), :], 0.0) * entered

    def span_rows(start, count):
        return pl.ds(pl.multiple_of(start, count), count)

    def r_copy(o):
        x = mod(me_x + o, side)
        return pltpu.make_async_remote_copy(
            src_ref=r_acc.at[span_rows(x * group, group)], dst_ref=r_in.at[o - 1],
            send_sem=r_ss.at[o - 1], recv_sem=r_rs.at[o - 1], device_id=at_xy(x, me_y),
        )

    def w_copy(o, x):
        y = mod(me_y + o, side)
        return pltpu.make_async_remote_copy(
            src_ref=w_acc.at[span_rows((x * side + y) * block, block)], dst_ref=w_in.at[o - 1, x],
            send_sem=w_ss.at[o - 1, x], recv_sem=w_rs.at[o - 1, x], device_id=at_xy(me_x, y),
        )

    def r_copy2(o):
        y = mod(me_y + o, side)
        return pltpu.make_async_remote_copy(
            src_ref=r_acc.at[span_rows((me_x * side + y) * block, block)], dst_ref=r_in2.at[o - 1],
            send_sem=r2_ss.at[o - 1], recv_sem=r2_rs.at[o - 1], device_id=at_xy(me_x, y),
        )

    def w_copy2(o):
        x = mod(me_x + o, side)
        return pltpu.make_async_remote_copy(
            src_ref=w_acc.at[span_rows((x * side + me_y) * block, block)], dst_ref=w_in2.at[o - 1],
            send_sem=w2_ss.at[o - 1], recv_sem=w2_rs.at[o - 1], device_id=at_xy(x, me_y),
        )

    def key_grads(c):
        rows = rows_of(c)
        column = doc_col[rows, :]
        half_row = half[pl.ds(c, 1), :]
        before, after = previous_doc(c), next_doc(c)
        sh, sl = two_parts(state_at(c, before) * half_row)
        sphi[c], splo[c] = sh, sl
        bh, bl = two_parts(back_at(c + 1, after) * half_row)
        bphi[c], bplo[c] = bh, bl
        to_read = dot_nt(ghi[rows, :], sh) + dot_nt(ghi[rows, :], sl) + dot_nt(glo[rows, :], sh)
        to_write = dot_nt(xhi[rows, :], bh) + dot_nt(xhi[rows, :], bl) + dot_nt(xlo[rows, :], bh)
        to_read = jnp.where(column == before, to_read, 0.0)
        to_write = jnp.where(column == after, to_write, 0.0)
        r_acc[rows, :] += to_read
        w_acc[rows, :] += to_write

    @pl.loop(0, side)
    def _(i):
        x = mod(me_x + 1 + i, side)
        pl.loop(0, chunks // side, unroll=True)(lambda k: key_grads(x * (chunks // side) + k))

        @pl.when(i < side - 1)
        def _():
            r_copy(i + 1).start()

        for o in range(1, side):
            w_copy(o, x).start()

    def rest(c):
        rows = rows_of(c)
        column = doc_col[rows, :]
        docs = doc_row(c)
        before, after, last = previous_doc(c), next_doc(c), docs[:, q - 1:]
        reads = jnp.where(column == before, r_ref[rows, :].astype(F32), 0.0).astype(BF16)
        writes = jnp.where(column == after, w_ref[rows, :].astype(F32), 0.0).astype(BF16)
        out = out_acc[rows, :] + dot_nn(reads, sphi[c]) + dot_nn(reads, splo[c])
        val = val_acc[rows, :] + dot_nn(writes, bphi[c]) + dot_nn(writes, bplo[c])
        vg_ref[rows, :] = (scale[rows, :] * val).astype(BF16)
        g_scaled = ghi[rows, :].astype(F32) + glo[rows, :].astype(F32)
        x_scaled = xhi[rows, :].astype(F32) + xlo[rows, :].astype(F32)
        high, low = two_parts(x_scaled * val)
        at_write = dot_nt(of_head16, high) + dot_nt(of_head16, low)
        high, low = two_parts(g_scaled * out)
        at_read = dot_nt(of_head16, high) + dot_nt(of_head16, low)
        lower = (jnp.concatenate([column] * doc_rows, axis=1) == docs) & (square_rows >= square_cols)
        later = stacked_dot(at_read - at_write, lower.astype(F32).astype(BF16))
        crossing = jnp.sum(state_at(c + 1, last) * back_at(c + 1, after), axis=0, keepdims=True)
        crossing = jnp.sum(of_head * crossing, axis=1, keepdims=True)
        crossing = jnp.where(last == after, crossing, 0.0)
        later = later + jnp.where(docs == last, crossing, 0.0)
        sg_ref[:, rows] = at_write / step_ref[:, rows] - rate * later

    later_from = (5 * chunks) // 8
    pl.loop(0, later_from)(rest)
    for o in range(1, side):
        r_copy(o).wait_recv()

        @pl.loop(0, side)
        def _(x):
            w_copy(o, x).wait_recv()

    for o in range(side):
        y = mod(me_y + o, side)
        rows = span_rows((me_x * side + y) * block, block)
        held = r_acc[rows, :]
        for k in range(side - 1):
            held = held + r_in[k, span_rows(y * block, block), :]
        r_acc[rows, :] = held
        if o > 0:
            r_copy2(o).start()
        x = mod(me_x + o, side)
        rows = span_rows((x * side + me_y) * block, block)
        held = w_acc[rows, :]
        for k in range(side - 1):
            held = held + w_in[k, x]
        w_acc[rows, :] = held
        if o > 0:
            w_copy2(o).start()
    pl.loop(later_from, chunks)(rest)
    mine_rows = span_rows(me * block, block)
    read_total, write_total = r_acc[mine_rows, :], w_acc[mine_rows, :]
    for o in range(1, side):
        r_copy2(o).wait_recv()
        read_total = read_total + r_in2[o - 1]
        w_copy2(o).wait_recv()
        write_total = write_total + w_in2[o - 1]
    wg_ref[...] = write_total
    rg_ref[...] = read_total
    for far in (1, 2):
        if far < n_z:

            @pl.when(me_z + far < n_z)
            def _():
                z_copy(0, far).wait_send()

            @pl.when(me_z - far >= 0)
            def _():
                z_copy(1, far).wait_send()

    for o in range(1, side):
        r_copy(o).wait_send()
        r_copy2(o).wait_send()
        w_copy2(o).wait_send()

        @pl.loop(0, side)
        def _(x):
            w_copy(o, x).wait_send()


def shards(mesh_shape, values, step_sizes, decay_rates, write_keys, read_keys, doc_ids, out_grad):
    n_ctx, n_head = mesh_shape
    length, width = values.shape
    heads = decay_rates.shape[0]
    states = write_keys.shape[1]
    chunks = length // QCHUNK
    block = length // n_head
    side = math.isqrt(n_head)
    vmem = pl.BlockSpec(memory_space=pltpu.VMEM)
    wide16 = pltpu.VMEM((length, width), BF16)
    wide32 = pltpu.VMEM((length, width), F32)
    def messages(count):
        return pltpu.VMEM((count, states + 8, width // 2), F32)

    def semaphores(*shape):
        return [pltpu.SemaphoreType.DMA(shape)] * 2

    others = max(side - 1, 1)
    value_grad, step_grad, write_grad, read_grad = pl.pallas_call(
        partial(kernel, n_ctx, n_head),
        out_shape=(
            jax.ShapeDtypeStruct((length, width), BF16),
            jax.ShapeDtypeStruct((heads, length), F32),
            jax.ShapeDtypeStruct((block, states), F32),
            jax.ShapeDtypeStruct((block, states), F32),
        ),
        in_specs=[vmem, vmem, vmem, pl.BlockSpec(memory_space=pltpu.SMEM), vmem, vmem, vmem],
        out_specs=(vmem, vmem, vmem, vmem),
        scratch_shapes=[
            wide16, wide16, wide16, wide16, wide32, wide32, wide32,
            pltpu.VMEM((length, 128), F32),
            pltpu.VMEM((length, states), F32),
            pltpu.VMEM((length, states), F32),
            pltpu.VMEM((others, length // side, states), F32),
            pltpu.VMEM((others, side, block, states), F32),
            pltpu.VMEM((others, block, states), F32),
            pltpu.VMEM((others, block, states), F32),
            pltpu.VMEM((chunks + 1, states, width), F32),
            pltpu.VMEM((chunks + 1, states, width), F32),
            pltpu.VMEM((chunks, width), F32),
            pltpu.VMEM((chunks + 1, width), F32),
            pltpu.VMEM((chunks + 1, width), F32),
            pltpu.VMEM((chunks, states, width), BF16),
            pltpu.VMEM((chunks, states, width), BF16),
            pltpu.VMEM((chunks, states, width), BF16),
            pltpu.VMEM((chunks, states, width), BF16),
            messages(2), messages(2), messages(1), messages(1), messages(1), messages(1),
            messages(2), messages(2), messages(1), messages(1), messages(2), messages(2),
            *semaphores(2), *semaphores(2, 2), *semaphores(2),
            *semaphores(others), *semaphores(others, side), *semaphores(others), *semaphores(others),
        ],
        compiler_params=pltpu.CompilerParams(
            collective_id=0, has_side_effects=True, vmem_limit_bytes=60 * 2**20
        ),
    )(
        values, out_grad, step_sizes.T, decay_rates, write_keys, read_keys,
        doc_ids.reshape(length // 128, 128),
    )
    return value_grad, step_grad.T, write_grad, read_grad


def solution(mesh):
    return jax.shard_map(
        partial(shards, (mesh.shape["ctx"], mesh.shape["head"])),
        mesh=mesh,
        in_specs=(
            P("ctx", "head"),
            P("ctx", "head"),
            P("head"),
            P("ctx", None),
            P("ctx", None),
            P("ctx"),
            P("ctx", "head"),
        ),
        out_specs=(
            P("ctx", "head"),
            P("ctx", "head"),
            P(("ctx", "head"), None),
            P(("ctx", "head"), None),
        ),
        check_vma=False,
    )
```

```python
import math
from functools import partial

import jax
import jax.numpy as jnp
from jax import lax
from jax.experimental import pallas as pl
from jax.experimental.pallas import tpu as pltpu
from jax.sharding import PartitionSpec as P

QCHUNK = 256
F32 = jnp.float32
BF16 = jnp.bfloat16


def two_parts(value):
    high = value.astype(BF16)
    return high, (value - high.astype(F32)).astype(BF16)


def three_parts(value):
    high = value.astype(BF16)
    rest = value - high.astype(F32)
    middle = rest.astype(BF16)
    return high, middle, (rest - middle.astype(F32)).astype(BF16)


def dot(left, right, contract):
    return lax.dot_general(left, right, ((contract[:1], contract[1:]), ((), ())), preferred_element_type=F32)


def dot_nn(left, right):
    return dot(left, right, (1, 0))


def dot_nt(left, right):
    return dot(left, right, (1, 1))


def dot_tn(left, right):
    return dot(left, right, (0, 0))


def mod(value, count):
    return lax.rem(value + count, count)


def kernel(
    n_ctx, n_head, x_hbm, g_hbm, step_ref, rate_ref, w_hbm, r_hbm, doc_ref,
    vg_ref, sg_ref, wg_ref, rg_ref,
    x_ref, g_ref, w_ref, r_ref, in_sems, u_parts, v_parts, grows, shrinks, entry,
    xhi, xlo, ghi, glo, scale, out_acc, val_acc, doc_col,
    r_acc, w_acc, r_mid, w_mid, r_in, w_in, r_in2, w_in2,
    state, back, half, phi_f, phi_b, sphi, splo, bphi, bplo,
    e_out, b_out, e_sib, b_sib, f_out, k_out, f_in, k_in, s_out, g_out, s_in, g_in,
    sib_ss, sib_rs, z_ss, z_rs, last_ss, last_rs,
    ra_ss, ra_rs, wa_ss, wa_rs, r_ss, r_rs, w_ss, w_rs, r2_ss, r2_rs, w2_ss, w2_rs,
):
    length, width = x_hbm.shape
    heads = step_ref.shape[0]
    head_size = width // heads
    states = w_hbm.shape[1]
    q = QCHUNK
    chunks = length // q
    side = math.isqrt(n_head)
    n_z = n_ctx // 2
    group = length // side
    block = length // n_head
    lanes = 128
    doc_rows = q // lanes
    hw = width // 2
    me_ctx, me = lax.axis_index("ctx"), lax.axis_index("head")
    me_z, core = me_ctx // 2, lax.rem(me_ctx, 2)
    me_x, me_y = me // side, lax.rem(me, side)

    def at_z(z):
        return {"ctx": z * 2 + core}

    def at_xy(x, y):
        return {"head": x * side + y}

    sibling = {"ctx": me_ctx + 1 - 2 * core}

    def put(ref, which, value, span, doc):
        ref[which, 0:states, :] = value
        ref[which, states:states + 1, :] = span
        ref[which, states + 1:states + 2, :] = jnp.broadcast_to(doc, (1, hw))

    def arrivals(c):
        rows = pl.ds(pl.multiple_of(c * q, q), q)
        pairs = ((g_hbm, g_ref), (x_hbm, x_ref), (w_hbm, w_ref), (r_hbm, r_ref))
        return [
            pltpu.make_async_copy(src.at[rows], dst.at[rows], in_sems.at[k, c])
            for k, (src, dst) in enumerate(pairs)
        ]

    @pl.loop(0, chunks)
    def _(c):
        for copy in arrivals(c):
            copy.start()

    for far in range(2):
        for ref in (f_in, k_in):
            put(ref, far, jnp.zeros((states, hw), F32), jnp.zeros((1, hw), F32), jnp.full((1, 1), -1.0, F32))

    barrier = pltpu.get_barrier_semaphore()
    pl.semaphore_signal(barrier, inc=1, device_id=sibling)
    for o in range(1, n_z):
        pl.semaphore_signal(barrier, inc=1, device_id=at_z(mod(me_z + o, n_z)))
    for o in range(1, side):
        pl.semaphore_signal(barrier, inc=1, device_id=at_xy(mod(me_x + o, side), me_y))
        pl.semaphore_signal(barrier, inc=1, device_id=at_xy(me_x, mod(me_y + o, side)))

    head_rows = lax.broadcasted_iota(jnp.int32, (heads, width), 0)
    head_lanes = lax.broadcasted_iota(jnp.int32, (heads, width), 1)
    of_head = jnp.where(head_lanes // head_size == head_rows, 1.0, 0.0)
    of_head16 = of_head.astype(BF16)
    spread3 = jnp.concatenate([of_head] * 3, axis=0).astype(BF16)
    square_rows = lax.broadcasted_iota(jnp.int32, (q, q), 0)
    square_cols = lax.broadcasted_iota(jnp.int32, (q, q), 1)
    rate = jnp.zeros((heads, 1), F32)
    rate_row = lax.broadcasted_iota(jnp.int32, (heads, 1), 0)
    for h in range(heads):
        rate = jnp.where(rate_row == h, rate_ref[h], rate)

    def rows_of(c):
        return pl.ds(pl.multiple_of(c * q, q), q)

    def doc_row(c):
        return jnp.concatenate(
            [doc_ref[pl.ds(c * doc_rows + k, 1), :] for k in range(doc_rows)], axis=1
        ).astype(F32)

    def first_doc(c):
        return doc_ref[pl.ds(c * doc_rows, 1), 0:1].astype(F32)

    def last_doc(c):
        return doc_ref[pl.ds(c * doc_rows + doc_rows - 1, 1), lanes - 1:lanes].astype(F32)

    def to_lanes(column):
        return jnp.sum(of_head * column, axis=0, keepdims=True)

    def stacked_parts(value):
        return jnp.concatenate([p.astype(F32) for p in three_parts(value)], axis=0).astype(BF16)

    def stacked_dot(value, right):
        made = dot_nn(stacked_parts(value), right)
        count = value.shape[0]
        return made[:count] + made[count:2 * count] + made[2 * count:]

    all_steps = jnp.concatenate([step_ref[:, c * q:(c + 1) * q] for c in range(chunks)], axis=0)
    all_rates = jnp.concatenate([rate] * chunks, axis=0)
    decay = stacked_dot(-all_steps * all_rates, (square_rows <= square_cols).astype(F32).astype(BF16))
    whole = decay[:, q - 1:q]
    from_middle = decay - 0.5 * whole
    grow, shrink = jnp.exp(from_middle), jnp.exp(-from_middle) * all_steps
    grows[...], shrinks[...] = grow, shrink
    total = jnp.zeros((heads, 1), F32)
    for c in range(chunks):
        of_chunk = slice(c * heads, (c + 1) * heads)
        u_parts[c] = stacked_parts(grow[of_chunk])
        v_parts[c] = stacked_parts(shrink[of_chunk])
        half[c:c + 1, :] = to_lanes(jnp.exp(0.5 * whole[of_chunk]))
        phi_f[c:c + 1, :] = to_lanes(jnp.exp(total))
        total = total + whole[of_chunk]

    state[0] = jnp.zeros((states, width), F32)
    back[chunks] = jnp.zeros((states, width), F32)

    def local_states(c):
        rows = rows_of(c)
        for copy in arrivals(c):
            copy.wait()
        high, low = two_parts(g_ref[rows, :].astype(F32) * dot_tn(u_parts[c], spread3))
        ghi[rows, :], glo[rows, :] = high, low
        x_scale = dot_tn(v_parts[c], spread3)
        scale[rows, :] = x_scale
        xh, xl = two_parts(x_ref[rows, :].astype(F32) * x_scale)
        xhi[rows, :], xlo[rows, :] = xh, xl
        docs = doc_row(c)
        column = jnp.transpose(jnp.broadcast_to(docs, (lanes, q)))
        doc_col[rows, :] = column
        half_row = half[pl.ds(c, 1), :]
        w_last = jnp.where(column == docs[:, q - 1:], w_ref[rows, :].astype(F32), 0.0).astype(BF16)
        r_first = jnp.where(column == docs[:, :1], r_ref[rows, :].astype(F32), 0.0).astype(BF16)
        made = (dot_tn(w_last, xh) + dot_tn(w_last, xl)) * half_row
        before = last_doc(jnp.maximum(c - 1, 0))
        kept = jnp.where(before == docs[:, q - 1:], half_row * half_row, 0.0)
        state[c + 1] = made + kept * state[c]
        made = (dot_tn(r_first, high) + dot_tn(r_first, low)) * half_row
        back[c] = made
        reached = jnp.where(docs[:, :1] == first_doc(0), phi_f[pl.ds(c, 1), :], 0.0)
        entry[...] = jnp.where(c == 0, made, entry[...] + reached * made)

    pl.loop(0, chunks, unroll=2)(local_states)
    phi_f[pl.ds(chunks, 1), :] = to_lanes(jnp.exp(total))
    whole_row = to_lanes(total)
    first_here, last_here = first_doc(0), last_doc(chunks - 1)

    def span_of(ref, which):
        return ref[which, states:states + 1, :]

    def doc_of(ref, which):
        return ref[which, states + 1:states + 2, :]

    def value_of(ref, which):
        return ref[which, 0:states, :]

    def joined(near, near_doc, near_span, far, far_doc):
        return near + jnp.where(near_doc == far_doc, jnp.exp(near_span), 0.0) * far

    def sib_copy(k, src, dst, ss, rs):
        return pltpu.make_async_remote_copy(
            src_ref=src, dst_ref=dst, send_sem=ss.at[k], recv_sem=rs.at[k], device_id=sibling
        )

    def z_copy(k, far):
        src, dst, to = (f_out, f_in, me_z + far) if k == 0 else (k_out, k_in, me_z - far)
        return pltpu.make_async_remote_copy(
            src_ref=src.at[0], dst_ref=dst.at[far - 1], send_sem=z_ss.at[k, far - 1],
            recv_sem=z_rs.at[k, far - 1], device_id=at_z(to),
        )

    def same_doc(c, rows):
        return jnp.concatenate([doc_col[rows, :]] * doc_rows, axis=1) == doc_row(c)

    def pairs(c):
        rows = rows_of(c)
        reads, writes = r_ref[rows, :], w_ref[rows, :]
        lower = same_doc(c, rows) & (square_rows >= square_cols)
        xh, xl, gh, gl = xhi[rows, :], xlo[rows, :], ghi[rows, :], glo[rows, :]
        made = dot_nt(gh, xh) + dot_nt(gh, xl) + dot_nt(gl, xh)
        high, low = two_parts(jnp.where(lower, made, 0.0))
        r_acc[rows, :] = dot_nn(high, writes) + dot_nn(low, writes)
        w_acc[rows, :] = jnp.transpose(dot_tn(reads, high) + dot_tn(reads, low))

    def within(c):
        rows = rows_of(c)
        reads, writes = r_ref[rows, :], w_ref[rows, :]
        same = same_doc(c, rows)
        lower = same & (square_rows >= square_cols)
        upper = same & (square_rows <= square_cols)
        xh, xl, gh, gl = xhi[rows, :], xlo[rows, :], ghi[rows, :], glo[rows, :]
        high, low = two_parts(jnp.where(lower, dot_nt(reads, writes), 0.0))
        out_acc[rows, :] = dot_nn(high, xh) + dot_nn(high, xl) + dot_nn(low, xh)
        high, low = two_parts(jnp.where(upper, dot_nt(writes, reads), 0.0))
        val_acc[rows, :] = dot_nn(high, gh) + dot_nn(high, gl) + dot_nn(low, gh)

    for k in range(2):
        lane = slice(k * hw, (k + 1) * hw)
        put(e_out, k, state[chunks][:, lane], whole_row[:, lane], last_here)
        put(b_out, k, entry[:, lane], whole_row[:, lane], first_here)
    pl.semaphore_wait(barrier, 1 + n_z - 1 + 2 * (side - 1))
    sib_copies = (
        sib_copy(0, e_out.at[1 - core], e_sib.at[0], sib_ss, sib_rs),
        sib_copy(1, b_out.at[1 - core], b_sib.at[0], sib_ss, sib_rs),
    )
    for copy in sib_copies:
        copy.start()
    phi_b[pl.ds(chunks, 1), :] = jnp.ones((1, width), F32)

    @pl.loop(0, chunks)
    def _(i):
        c = chunks - 1 - i
        half_row = half[pl.ds(c, 1), :]
        square = half_row * half_row
        kept = jnp.where(first_doc(jnp.minimum(c + 1, chunks - 1)) == first_doc(c), square, 0.0)
        back[c] = back[c] + kept * back[c + 1]
        phi_b[pl.ds(c, 1), :] = phi_b[pl.ds(c + 1, 1), :] * square

    first, early = chunks // 8, (3 * chunks) // 8
    for copy in sib_copies:
        copy.wait()
    low, mine, other = core == 0, core, 0
    e_low = jnp.where(low, value_of(e_out, mine), value_of(e_sib, other))
    e_high = jnp.where(low, value_of(e_sib, other), value_of(e_out, mine))
    b_low = jnp.where(low, value_of(b_out, mine), value_of(b_sib, other))
    b_high = jnp.where(low, value_of(b_sib, other), value_of(b_out, mine))
    span_low = jnp.where(low, span_of(e_out, mine), span_of(e_sib, other))
    span_high = jnp.where(low, span_of(e_sib, other), span_of(e_out, mine))
    last_low = jnp.where(low, doc_of(e_out, mine), doc_of(e_sib, other))
    last_high = jnp.where(low, doc_of(e_sib, other), doc_of(e_out, mine))
    first_low = jnp.where(low, doc_of(b_out, mine), doc_of(b_sib, other))
    first_high = jnp.where(low, doc_of(b_sib, other), doc_of(b_out, mine))
    put(f_out, 0, joined(e_high, last_high, span_high, e_low, last_low), span_low + span_high, last_high)
    put(k_out, 0, joined(b_low, first_low, span_low, b_high, first_high), span_low + span_high, first_low)
    for far in (1, 2):
        if far < n_z:

            @pl.when(me_z + far < n_z)
            def _():
                z_copy(0, far).start()

            @pl.when(me_z - far >= 0)
            def _():
                z_copy(1, far).start()

    pl.loop(0, chunks)(pairs)
    pl.loop(first, early)(within)
    for far in (1, 2):
        if far < n_z:

            @pl.when(me_z - far >= 0)
            def _():
                z_copy(0, far).wait_recv()

            @pl.when(me_z + far < n_z)
            def _():
                z_copy(1, far).wait_recv()

    s_chip = joined(value_of(f_in, 0), doc_of(f_in, 0), span_of(f_in, 0), value_of(f_in, 1), doc_of(f_in, 1))
    g_chip = joined(value_of(k_in, 0), doc_of(k_in, 0), span_of(k_in, 0), value_of(k_in, 1), doc_of(k_in, 1))
    s_high = joined(value_of(e_out, mine), last_low, span_low, s_chip, doc_of(f_in, 0))
    s_high = jnp.where(low, s_high, joined(value_of(e_sib, other), last_low, span_low, s_chip, doc_of(f_in, 0)))
    g_low = joined(value_of(b_sib, other), first_high, span_high, g_chip, doc_of(k_in, 0))
    g_low = jnp.where(low, g_low, joined(value_of(b_out, mine), first_high, span_high, g_chip, doc_of(k_in, 0)))
    s_doc_low, s_doc_high = doc_of(f_in, 0), last_low
    g_doc_low, g_doc_high = first_high, doc_of(k_in, 0)
    put(s_out, 0, jnp.where(low, s_high, s_chip), span_low, jnp.where(low, s_doc_high, s_doc_low))
    put(g_out, 0, jnp.where(low, g_chip, g_low), span_low, jnp.where(low, g_doc_high, g_doc_low))
    last_copies = (
        sib_copy(0, s_out.at[0], s_in.at[mine], last_ss, last_rs),
        sib_copy(1, g_out.at[0], g_in.at[mine], last_ss, last_rs),
    )
    for copy in last_copies:
        copy.start()
    put(s_in, mine, jnp.where(low, s_chip, s_high), span_low, jnp.where(low, s_doc_low, s_doc_high))
    put(g_in, mine, jnp.where(low, g_low, g_chip), span_low, jnp.where(low, g_doc_low, g_doc_high))
    pl.loop(0, first)(within)
    for copy in last_copies:
        copy.wait()

    doc_before, doc_after = doc_of(s_in, 0)[:, :1], doc_of(g_in, 0)[:, :1]

    def previous_doc(c):
        return jnp.where(c == 0, doc_before, last_doc(jnp.maximum(c - 1, 0)))

    def next_doc(c):
        return jnp.where(c == chunks - 1, doc_after, first_doc(jnp.minimum(c + 1, chunks - 1)))

    def state_at(k, doc):
        entered = jnp.concatenate([value_of(s_in, 0), value_of(s_in, 1)], axis=1)
        return state[k] + jnp.where(doc == doc_before, phi_f[pl.ds(k, 1), :], 0.0) * entered

    def back_at(k, doc):
        entered = jnp.concatenate([value_of(g_in, 0), value_of(g_in, 1)], axis=1)
        return back[k] + jnp.where(doc == doc_after, phi_b[pl.ds(k, 1), :], 0.0) * entered

    def span_rows(start, count):
        return pl.ds(pl.multiple_of(start, count), count)

    def to_side(near):
        return side - 1 if near else 1

    def r_relay(near):
        start = mod(me_x + side // 2, side) * group + near * (group // 2)
        return pltpu.make_async_remote_copy(
            src_ref=r_acc.at[span_rows(start, group // 2)], dst_ref=r_mid.at[near],
            send_sem=ra_ss.at[near], recv_sem=ra_rs.at[near],
            device_id=at_xy(mod(me_x + to_side(near), side), me_y),
        )

    def r_copy(near):
        x = mod(me_x + to_side(near), side)
        return pltpu.make_async_remote_copy(
            src_ref=r_acc.at[span_rows(x * group, group)], dst_ref=r_in.at[near],
            send_sem=r_ss.at[near], recv_sem=r_rs.at[near], device_id=at_xy(x, me_y),
        )

    def w_relay(near, x):
        start = (x * side + mod(me_y + side // 2, side)) * block + near * (block // 2)
        return pltpu.make_async_remote_copy(
            src_ref=w_acc.at[span_rows(start, block // 2)], dst_ref=w_mid.at[near, x],
            send_sem=wa_ss.at[near, x], recv_sem=wa_rs.at[near, x],
            device_id=at_xy(me_x, mod(me_y + to_side(near), side)),
        )

    def w_copy(near, x):
        y = mod(me_y + to_side(near), side)
        return pltpu.make_async_remote_copy(
            src_ref=w_acc.at[span_rows((x * side + y) * block, block)], dst_ref=w_in.at[near, x],
            send_sem=w_ss.at[near, x], recv_sem=w_rs.at[near, x], device_id=at_xy(me_x, y),
        )

    def r_copy2(o):
        y = mod(me_y + o, side)
        return pltpu.make_async_remote_copy(
            src_ref=r_acc.at[span_rows((me_x * side + y) * block, block)], dst_ref=r_in2.at[o - 1],
            send_sem=r2_ss.at[o - 1], recv_sem=r2_rs.at[o - 1], device_id=at_xy(me_x, y),
        )

    def w_copy2(o):
        x = mod(me_x + o, side)
        return pltpu.make_async_remote_copy(
            src_ref=w_acc.at[span_rows((x * side + me_y) * block, block)], dst_ref=w_in2.at[o - 1],
            send_sem=w2_ss.at[o - 1], recv_sem=w2_rs.at[o - 1], device_id=at_xy(x, me_y),
        )

    def key_grads(c):
        rows = rows_of(c)
        column = doc_col[rows, :]
        half_row = half[pl.ds(c, 1), :]
        before, after = previous_doc(c), next_doc(c)
        sh, sl = two_parts(state_at(c, before) * half_row)
        sphi[c], splo[c] = sh, sl
        bh, bl = two_parts(back_at(c + 1, after) * half_row)
        bphi[c], bplo[c] = bh, bl
        pair = dot_nt(ghi[rows, :], jnp.concatenate([sh, sl], axis=0))
        to_read = pair[:, :states] + pair[:, states:] + dot_nt(glo[rows, :], sh)
        pair = dot_nt(xhi[rows, :], jnp.concatenate([bh, bl], axis=0))
        to_write = pair[:, :states] + pair[:, states:] + dot_nt(xlo[rows, :], bh)
        to_read = jnp.where(column == before, to_read, 0.0)
        to_write = jnp.where(column == after, to_write, 0.0)
        r_acc[rows, :] += to_read
        w_acc[rows, :] += to_write

    both = (0, 1)

    @pl.loop(0, side)
    def _(i):
        o = jnp.where(i == 0, side // 2, jnp.where(i == 1, 1, jnp.where(i == 2, side - 1, 0)))
        x = mod(me_x + o, side)
        pl.loop(0, chunks // side, unroll=True)(lambda k: key_grads(x * (chunks // side) + k))

        @pl.when(i == 0)
        def _():
            for near in both:
                r_relay(near).start()

        for near in both:
            w_relay(near, x).start()

    def per_head(value):
        high, low = two_parts(value)
        return dot_nt(of_head16, high) + dot_nt(of_head16, low)

    def rest(c):
        rows = rows_of(c)
        column = doc_col[rows, :]
        docs = doc_row(c)
        before, after, last = previous_doc(c), next_doc(c), docs[:, q - 1:]
        reads = jnp.where(column == before, r_ref[rows, :].astype(F32), 0.0).astype(BF16)
        writes = jnp.where(column == after, w_ref[rows, :].astype(F32), 0.0).astype(BF16)
        out = out_acc[rows, :] + dot_nn(jnp.concatenate([reads, reads], axis=1), jnp.concatenate([sphi[c], splo[c]], axis=0))
        val = val_acc[rows, :] + dot_nn(jnp.concatenate([writes, writes], axis=1), jnp.concatenate([bphi[c], bplo[c]], axis=0))
        vg_ref[rows, :] = (scale[rows, :] * val).astype(BF16)
        of_chunk = pl.ds(pl.multiple_of(c * heads, heads), heads)
        at_write = shrinks[of_chunk, :] * per_head(x_ref[rows, :].astype(F32) * val)
        at_read = grows[of_chunk, :] * per_head(g_ref[rows, :].astype(F32) * out)
        lower = (jnp.concatenate([column] * doc_rows, axis=1) == docs) & (square_rows >= square_cols)
        later = stacked_dot(at_read - at_write, lower.astype(F32).astype(BF16))
        crossing = jnp.sum(state_at(c + 1, last) * back_at(c + 1, after), axis=0, keepdims=True)
        crossing = jnp.sum(of_head * crossing, axis=1, keepdims=True)
        crossing = jnp.where(last == after, crossing, 0.0)
        later = later + jnp.where(docs == last, crossing, 0.0)
        sg_ref[:, rows] = at_write / step_ref[:, rows] - rate * later

    middle_at, late = (4 * chunks) // 8, (5 * chunks) // 8
    pl.loop(early, middle_at)(within)
    for near in both:
        r_relay(near).wait_recv()
        rows = span_rows(mod(me_x + to_side(near), side) * group + near * (group // 2), group // 2)
        r_acc[rows, :] += r_mid[near]
        r_copy(near).start()
    pl.loop(middle_at, late)(within)

    @pl.loop(0, side)
    def _(x):
        for near in both:
            w_relay(near, x).wait_recv()
            start = (x * side + mod(me_y + to_side(near), side)) * block + near * (block // 2)
            rows = span_rows(start, block // 2)
            w_acc[rows, :] += w_mid[near, x]
            w_copy(near, x).start()

    pl.loop(late, chunks)(within)
    later_from = chunks // 2
    pl.loop(0, later_from, unroll=2)(rest)
    for near in both:
        r_copy(near).wait_recv()

    @pl.loop(0, side)
    def _(x):
        for near in both:
            w_copy(near, x).wait_recv()

    for o in range(side):
        y = mod(me_y + o, side)
        rows = span_rows((me_x * side + y) * block, block)
        held = r_acc[rows, :]
        for k in both:
            held = held + r_in[k, span_rows(y * block, block), :]
        r_acc[rows, :] = held
        if o > 0:
            r_copy2(o).start()
        x = mod(me_x + o, side)
        rows = span_rows((x * side + me_y) * block, block)
        held = w_acc[rows, :]
        for k in both:
            held = held + w_in[k, x]
        w_acc[rows, :] = held
        if o > 0:
            w_copy2(o).start()
    pl.loop(later_from, chunks, unroll=2)(rest)
    mine_rows = span_rows(me * block, block)
    read_total, write_total = r_acc[mine_rows, :], w_acc[mine_rows, :]
    for o in range(1, side):
        r_copy2(o).wait_recv()
        read_total = read_total + r_in2[o - 1]
        w_copy2(o).wait_recv()
        write_total = write_total + w_in2[o - 1]
    wg_ref[...] = write_total
    rg_ref[...] = read_total
    for far in (1, 2):
        if far < n_z:

            @pl.when(me_z + far < n_z)
            def _():
                z_copy(0, far).wait_send()

            @pl.when(me_z - far >= 0)
            def _():
                z_copy(1, far).wait_send()

    for near in both:
        r_relay(near).wait_send()
        r_copy(near).wait_send()

    @pl.loop(0, side)
    def _(x):
        for near in both:
            w_relay(near, x).wait_send()
            w_copy(near, x).wait_send()

    for o in range(1, side):
        r_copy2(o).wait_send()
        w_copy2(o).wait_send()


def shards(mesh_shape, values, step_sizes, decay_rates, write_keys, read_keys, doc_ids, out_grad):
    n_ctx, n_head = mesh_shape
    length, width = values.shape
    heads = decay_rates.shape[0]
    states = write_keys.shape[1]
    chunks = length // QCHUNK
    block = length // n_head
    side = math.isqrt(n_head)
    vmem, hbm = pl.BlockSpec(memory_space=pltpu.VMEM), pl.BlockSpec(memory_space=pl.ANY)
    wide16 = pltpu.VMEM((length, width), BF16)
    wide32 = pltpu.VMEM((length, width), F32)
    def messages(count):
        return pltpu.VMEM((count, states + 8, width // 2), F32)

    def semaphores(*shape):
        return [pltpu.SemaphoreType.DMA(shape)] * 2

    others = max(side - 1, 1)
    value_grad, step_grad, write_grad, read_grad = pl.pallas_call(
        partial(kernel, n_ctx, n_head),
        out_shape=(
            pltpu.VMEM((length, width), BF16),
            pltpu.VMEM((heads, length), F32),
            pltpu.VMEM((block, states), F32),
            pltpu.VMEM((block, states), F32),
        ),
        in_specs=[hbm, hbm, vmem, pl.BlockSpec(memory_space=pltpu.SMEM), hbm, hbm, vmem],
        out_specs=(vmem, vmem, vmem, vmem),
        scratch_shapes=[
            wide16, wide16, pltpu.VMEM((length, states), BF16), pltpu.VMEM((length, states), BF16),
            pltpu.SemaphoreType.DMA((4, chunks)),
            pltpu.VMEM((chunks, 3 * heads, QCHUNK), BF16), pltpu.VMEM((chunks, 3 * heads, QCHUNK), BF16),
            pltpu.VMEM((chunks * heads, QCHUNK), F32), pltpu.VMEM((chunks * heads, QCHUNK), F32),
            pltpu.VMEM((states, width), F32),
            wide16, wide16, wide16, wide16, wide32, wide32, wide32,
            pltpu.VMEM((length, 128), F32),
            pltpu.VMEM((length, states), F32),
            pltpu.VMEM((length, states), F32),
            pltpu.VMEM((2, length // side // 2, states), F32),
            pltpu.VMEM((2, side, block // 2, states), F32),
            pltpu.VMEM((2, length // side, states), F32),
            pltpu.VMEM((2, side, block, states), F32),
            pltpu.VMEM((others, block, states), F32),
            pltpu.VMEM((others, block, states), F32),
            pltpu.VMEM((chunks + 1, states, width), F32),
            pltpu.VMEM((chunks + 1, states, width), F32),
            pltpu.VMEM((chunks, width), F32),
            pltpu.VMEM((chunks + 1, width), F32),
            pltpu.VMEM((chunks + 1, width), F32),
            pltpu.VMEM((chunks, states, width), BF16),
            pltpu.VMEM((chunks, states, width), BF16),
            pltpu.VMEM((chunks, states, width), BF16),
            pltpu.VMEM((chunks, states, width), BF16),
            messages(2), messages(2), messages(1), messages(1), messages(1), messages(1),
            messages(2), messages(2), messages(1), messages(1), messages(2), messages(2),
            *semaphores(2), *semaphores(2, 2), *semaphores(2),
            *semaphores(2), *semaphores(2, side), *semaphores(2), *semaphores(2, side),
            *semaphores(others), *semaphores(others),
        ],
        compiler_params=pltpu.CompilerParams(
            collective_id=0, has_side_effects=True, vmem_limit_bytes=58 * 2**20
        ),
    )(
        values, out_grad, step_sizes.T, decay_rates, write_keys, read_keys,
        doc_ids.reshape(length // 128, 128),
    )
    return value_grad, step_grad.T, write_grad, read_grad


def solution(mesh):
    return jax.shard_map(
        partial(shards, (mesh.shape["ctx"], mesh.shape["head"])),
        mesh=mesh,
        in_specs=(
            P("ctx", "head"),
            P("ctx", "head"),
            P("head"),
            P("ctx", None),
            P("ctx", None),
            P("ctx"),
            P("ctx", "head"),
        ),
        out_specs=(
            P("ctx", "head"),
            P("ctx", "head"),
            P(("ctx", "head"), None),
            P(("ctx", "head"), None),
        ),
        check_vma=False,
    )
```

```python
import math
from functools import partial

import jax
import jax.numpy as jnp
from jax import lax
from jax.experimental import pallas as pl
from jax.experimental.pallas import tpu as pltpu
from jax.sharding import PartitionSpec as P

QCHUNK = 256
F32 = jnp.float32
BF16 = jnp.bfloat16


def two_parts(value):
    high = value.astype(BF16)
    return high, (value - high.astype(F32)).astype(BF16)


def three_parts(value):
    high = value.astype(BF16)
    rest = value - high.astype(F32)
    middle = rest.astype(BF16)
    return high, middle, (rest - middle.astype(F32)).astype(BF16)


def dot(left, right, contract):
    return lax.dot_general(left, right, ((contract[:1], contract[1:]), ((), ())), preferred_element_type=F32)


def dot_nn(left, right):
    return dot(left, right, (1, 0))


def dot_nt(left, right):
    return dot(left, right, (1, 1))


def dot_tn(left, right):
    return dot(left, right, (0, 0))


def mod(value, count):
    return lax.rem(value + count, count)


def kernel(
    n_ctx, n_head, x_hbm, g_hbm, step_hbm, rate_ref, w_hbm, r_hbm, doc_hbm,
    vg_ref, sg_ref, kg_ref,
    x_ref, g_ref, w_ref, r_ref, step_ref, doc_ref, small_sems, in_sems, u_parts, v_parts, grows, shrinks, entry,
    xhi, xlo, ghi, glo, scale, out_acc, val_acc, doc_col,
    r_acc, w_acc, r_mid, w_mid, r_in, w_in, r_in2, w_in2,
    state, back, half, phi_f, phi_b, sphi, splo, bphi, bplo,
    e_out, b_out, e_sib, b_sib, f_out, k_out, f_in, k_in, s_out, g_out, s_in, g_in,
    sib_ss, sib_rs, z_ss, z_rs, last_ss, last_rs,
    ra_ss, ra_rs, wa_ss, wa_rs, r_ss, r_rs, w_ss, w_rs, r2_ss, r2_rs, w2_ss, w2_rs,
):
    length, width = x_hbm.shape
    heads = step_hbm.shape[0]
    head_size = width // heads
    states = w_hbm.shape[1]
    q = QCHUNK
    chunks = length // q
    side = math.isqrt(n_head)
    n_z = n_ctx // 2
    group = length // side
    block = length // n_head
    lanes = 128
    doc_rows = q // lanes
    hw = width // 2
    me_ctx, me = lax.axis_index("ctx"), lax.axis_index("head")
    me_z, core = me_ctx // 2, lax.rem(me_ctx, 2)
    me_x, me_y = me // side, lax.rem(me, side)

    def at_z(z):
        return {"ctx": z * 2 + core}

    def at_xy(x, y):
        return {"head": x * side + y}

    sibling = {"ctx": me_ctx + 1 - 2 * core}

    def put(ref, which, value, span, doc):
        ref[which, 0:states, :] = value
        ref[which, states:states + 1, :] = span
        ref[which, states + 1:states + 2, :] = jnp.broadcast_to(doc, (1, hw))

    def arrivals(c):
        rows = pl.ds(pl.multiple_of(c * q, q), q)
        pairs = ((g_hbm, g_ref), (x_hbm, x_ref), (w_hbm, w_ref), (r_hbm, r_ref))
        return [
            pltpu.make_async_copy(src.at[rows], dst.at[rows], in_sems.at[k, c])
            for k, (src, dst) in enumerate(pairs)
        ]

    small = (
        pltpu.make_async_copy(step_hbm, step_ref, small_sems.at[0]),
        pltpu.make_async_copy(doc_hbm, doc_ref, small_sems.at[1]),
    )
    for copy in small:
        copy.start()

    @pl.loop(0, chunks)
    def _(c):
        for copy in arrivals(c):
            copy.start()

    for far in range(2):
        for ref in (f_in, k_in):
            put(ref, far, jnp.zeros((states, hw), F32), jnp.zeros((1, hw), F32), jnp.full((1, 1), -1.0, F32))

    barrier = pltpu.get_barrier_semaphore()
    pl.semaphore_signal(barrier, inc=1, device_id=sibling)
    for o in range(1, n_z):
        pl.semaphore_signal(barrier, inc=1, device_id=at_z(mod(me_z + o, n_z)))
    for o in range(1, side):
        pl.semaphore_signal(barrier, inc=1, device_id=at_xy(mod(me_x + o, side), me_y))
        pl.semaphore_signal(barrier, inc=1, device_id=at_xy(me_x, mod(me_y + o, side)))

    head_rows = lax.broadcasted_iota(jnp.int32, (heads, width), 0)
    head_lanes = lax.broadcasted_iota(jnp.int32, (heads, width), 1)
    of_head = jnp.where(head_lanes // head_size == head_rows, 1.0, 0.0)
    of_head16 = of_head.astype(BF16)
    spread3 = jnp.concatenate([of_head] * 3, axis=0).astype(BF16)
    square_rows = lax.broadcasted_iota(jnp.int32, (q, q), 0)
    square_cols = lax.broadcasted_iota(jnp.int32, (q, q), 1)
    rate = jnp.zeros((heads, 1), F32)
    rate_row = lax.broadcasted_iota(jnp.int32, (heads, 1), 0)
    for h in range(heads):
        rate = jnp.where(rate_row == h, rate_ref[h], rate)

    def rows_of(c):
        return pl.ds(pl.multiple_of(c * q, q), q)

    def doc_row(c):
        return jnp.concatenate(
            [doc_ref[pl.ds(c * doc_rows + k, 1), :] for k in range(doc_rows)], axis=1
        ).astype(F32)

    def first_doc(c):
        return doc_ref[pl.ds(c * doc_rows, 1), 0:1].astype(F32)

    def last_doc(c):
        return doc_ref[pl.ds(c * doc_rows + doc_rows - 1, 1), lanes - 1:lanes].astype(F32)

    def to_lanes(column):
        return jnp.sum(of_head * column, axis=0, keepdims=True)

    def stacked_parts(value):
        return jnp.concatenate([p.astype(F32) for p in three_parts(value)], axis=0).astype(BF16)

    def stacked_dot(value, right):
        made = dot_nn(stacked_parts(value), right)
        count = value.shape[0]
        return made[:count] + made[count:2 * count] + made[2 * count:]

    for copy in small:
        copy.wait()
    all_steps = jnp.concatenate([step_ref[:, c * q:(c + 1) * q] for c in range(chunks)], axis=0)
    all_rates = jnp.concatenate([rate] * chunks, axis=0)
    decay = stacked_dot(-all_steps * all_rates, (square_rows <= square_cols).astype(F32).astype(BF16))
    whole = decay[:, q - 1:q]
    from_middle = decay - 0.5 * whole
    grow, shrink = jnp.exp(from_middle), jnp.exp(-from_middle) * all_steps
    grows[...], shrinks[...] = grow, shrink
    total = jnp.zeros((heads, 1), F32)
    for c in range(chunks):
        of_chunk = slice(c * heads, (c + 1) * heads)
        u_parts[c] = stacked_parts(grow[of_chunk])
        v_parts[c] = stacked_parts(shrink[of_chunk])
        half[c:c + 1, :] = to_lanes(jnp.exp(0.5 * whole[of_chunk]))
        phi_f[c:c + 1, :] = to_lanes(jnp.exp(total))
        total = total + whole[of_chunk]

    state[0] = jnp.zeros((states, width), F32)
    back[chunks] = jnp.zeros((states, width), F32)

    def local_states(c):
        rows = rows_of(c)
        for copy in arrivals(c):
            copy.wait()
        high, low = two_parts(g_ref[rows, :].astype(F32) * dot_tn(u_parts[c], spread3))
        ghi[rows, :], glo[rows, :] = high, low
        x_scale = dot_tn(v_parts[c], spread3)
        scale[rows, :] = x_scale
        xh, xl = two_parts(x_ref[rows, :].astype(F32) * x_scale)
        xhi[rows, :], xlo[rows, :] = xh, xl
        docs = doc_row(c)
        column = jnp.transpose(jnp.broadcast_to(docs, (lanes, q)))
        doc_col[rows, :] = column
        half_row = half[pl.ds(c, 1), :]
        w_last = jnp.where(column == docs[:, q - 1:], w_ref[rows, :].astype(F32), 0.0).astype(BF16)
        r_first = jnp.where(column == docs[:, :1], r_ref[rows, :].astype(F32), 0.0).astype(BF16)
        made = (dot_tn(w_last, xh) + dot_tn(w_last, xl)) * half_row
        before = last_doc(jnp.maximum(c - 1, 0))
        kept = jnp.where(before == docs[:, q - 1:], half_row * half_row, 0.0)
        state[c + 1] = made + kept * state[c]
        made = (dot_tn(r_first, high) + dot_tn(r_first, low)) * half_row
        back[c] = made
        reached = jnp.where(docs[:, :1] == first_doc(0), phi_f[pl.ds(c, 1), :], 0.0)
        entry[...] = jnp.where(c == 0, made, entry[...] + reached * made)

    pl.loop(0, chunks, unroll=2)(local_states)
    phi_f[pl.ds(chunks, 1), :] = to_lanes(jnp.exp(total))
    whole_row = to_lanes(total)
    first_here, last_here = first_doc(0), last_doc(chunks - 1)

    def span_of(ref, which):
        return ref[which, states:states + 1, :]

    def doc_of(ref, which):
        return ref[which, states + 1:states + 2, :]

    def value_of(ref, which):
        return ref[which, 0:states, :]

    def joined(near, near_doc, near_span, far, far_doc):
        return near + jnp.where(near_doc == far_doc, jnp.exp(near_span), 0.0) * far

    def sib_copy(k, src, dst, ss, rs):
        return pltpu.make_async_remote_copy(
            src_ref=src, dst_ref=dst, send_sem=ss.at[k], recv_sem=rs.at[k], device_id=sibling
        )

    def z_copy(k, far):
        src, dst, to = (f_out, f_in, me_z + far) if k == 0 else (k_out, k_in, me_z - far)
        return pltpu.make_async_remote_copy(
            src_ref=src.at[0], dst_ref=dst.at[far - 1], send_sem=z_ss.at[k, far - 1],
            recv_sem=z_rs.at[k, far - 1], device_id=at_z(to),
        )

    def same_doc(c, rows):
        return jnp.concatenate([doc_col[rows, :]] * doc_rows, axis=1) == doc_row(c)

    def pairs(c):
        rows = rows_of(c)
        reads, writes = r_ref[rows, :], w_ref[rows, :]
        lower = same_doc(c, rows) & (square_rows >= square_cols)
        xh, xl, gh, gl = xhi[rows, :], xlo[rows, :], ghi[rows, :], glo[rows, :]
        made = dot_nt(gh, xh) + dot_nt(gh, xl) + dot_nt(gl, xh)
        high, low = two_parts(jnp.where(lower, made, 0.0))
        r_acc[rows, :] = dot_nn(high, writes) + dot_nn(low, writes)
        w_acc[rows, :] = jnp.transpose(dot_tn(reads, high) + dot_tn(reads, low))

    def within(c):
        rows = rows_of(c)
        reads, writes = r_ref[rows, :], w_ref[rows, :]
        same = same_doc(c, rows)
        lower = same & (square_rows >= square_cols)
        upper = same & (square_rows <= square_cols)
        xh, xl, gh, gl = xhi[rows, :], xlo[rows, :], ghi[rows, :], glo[rows, :]
        high, low = two_parts(jnp.where(lower, dot_nt(reads, writes), 0.0))
        out_acc[rows, :] = dot_nn(high, xh) + dot_nn(high, xl) + dot_nn(low, xh)
        high, low = two_parts(jnp.where(upper, dot_nt(writes, reads), 0.0))
        val_acc[rows, :] = dot_nn(high, gh) + dot_nn(high, gl) + dot_nn(low, gh)

    for k in range(2):
        lane = slice(k * hw, (k + 1) * hw)
        put(e_out, k, state[chunks][:, lane], whole_row[:, lane], last_here)
        put(b_out, k, entry[:, lane], whole_row[:, lane], first_here)
    pl.semaphore_wait(barrier, 1 + n_z - 1 + 2 * (side - 1))
    sib_copies = (
        sib_copy(0, e_out.at[1 - core], e_sib.at[0], sib_ss, sib_rs),
        sib_copy(1, b_out.at[1 - core], b_sib.at[0], sib_ss, sib_rs),
    )
    for copy in sib_copies:
        copy.start()
    phi_b[pl.ds(chunks, 1), :] = jnp.ones((1, width), F32)

    @pl.loop(0, chunks)
    def _(i):
        c = chunks - 1 - i
        half_row = half[pl.ds(c, 1), :]
        square = half_row * half_row
        kept = jnp.where(first_doc(jnp.minimum(c + 1, chunks - 1)) == first_doc(c), square, 0.0)
        back[c] = back[c] + kept * back[c + 1]
        phi_b[pl.ds(c, 1), :] = phi_b[pl.ds(c + 1, 1), :] * square

    first, early = chunks // 8, (3 * chunks) // 8
    for copy in sib_copies:
        copy.wait()
    low, mine, other = core == 0, core, 0
    e_low = jnp.where(low, value_of(e_out, mine), value_of(e_sib, other))
    e_high = jnp.where(low, value_of(e_sib, other), value_of(e_out, mine))
    b_low = jnp.where(low, value_of(b_out, mine), value_of(b_sib, other))
    b_high = jnp.where(low, value_of(b_sib, other), value_of(b_out, mine))
    span_low = jnp.where(low, span_of(e_out, mine), span_of(e_sib, other))
    span_high = jnp.where(low, span_of(e_sib, other), span_of(e_out, mine))
    last_low = jnp.where(low, doc_of(e_out, mine), doc_of(e_sib, other))
    last_high = jnp.where(low, doc_of(e_sib, other), doc_of(e_out, mine))
    first_low = jnp.where(low, doc_of(b_out, mine), doc_of(b_sib, other))
    first_high = jnp.where(low, doc_of(b_sib, other), doc_of(b_out, mine))
    put(f_out, 0, joined(e_high, last_high, span_high, e_low, last_low), span_low + span_high, last_high)
    put(k_out, 0, joined(b_low, first_low, span_low, b_high, first_high), span_low + span_high, first_low)
    for far in (1, 2):
        if far < n_z:

            @pl.when(me_z + far < n_z)
            def _():
                z_copy(0, far).start()

            @pl.when(me_z - far >= 0)
            def _():
                z_copy(1, far).start()

    pl.loop(0, chunks)(pairs)
    pl.loop(first, early)(within)
    for far in (1, 2):
        if far < n_z:

            @pl.when(me_z - far >= 0)
            def _():
                z_copy(0, far).wait_recv()

            @pl.when(me_z + far < n_z)
            def _():
                z_copy(1, far).wait_recv()

    s_chip = joined(value_of(f_in, 0), doc_of(f_in, 0), span_of(f_in, 0), value_of(f_in, 1), doc_of(f_in, 1))
    g_chip = joined(value_of(k_in, 0), doc_of(k_in, 0), span_of(k_in, 0), value_of(k_in, 1), doc_of(k_in, 1))
    s_high = joined(value_of(e_out, mine), last_low, span_low, s_chip, doc_of(f_in, 0))
    s_high = jnp.where(low, s_high, joined(value_of(e_sib, other), last_low, span_low, s_chip, doc_of(f_in, 0)))
    g_low = joined(value_of(b_sib, other), first_high, span_high, g_chip, doc_of(k_in, 0))
    g_low = jnp.where(low, g_low, joined(value_of(b_out, mine), first_high, span_high, g_chip, doc_of(k_in, 0)))
    s_doc_low, s_doc_high = doc_of(f_in, 0), last_low
    g_doc_low, g_doc_high = first_high, doc_of(k_in, 0)
    put(s_out, 0, jnp.where(low, s_high, s_chip), span_low, jnp.where(low, s_doc_high, s_doc_low))
    put(g_out, 0, jnp.where(low, g_chip, g_low), span_low, jnp.where(low, g_doc_high, g_doc_low))
    last_copies = (
        sib_copy(0, s_out.at[0], s_in.at[mine], last_ss, last_rs),
        sib_copy(1, g_out.at[0], g_in.at[mine], last_ss, last_rs),
    )
    for copy in last_copies:
        copy.start()
    put(s_in, mine, jnp.where(low, s_chip, s_high), span_low, jnp.where(low, s_doc_low, s_doc_high))
    put(g_in, mine, jnp.where(low, g_low, g_chip), span_low, jnp.where(low, g_doc_low, g_doc_high))
    pl.loop(0, first)(within)
    for copy in last_copies:
        copy.wait()

    doc_before, doc_after = doc_of(s_in, 0)[:, :1], doc_of(g_in, 0)[:, :1]

    def previous_doc(c):
        return jnp.where(c == 0, doc_before, last_doc(jnp.maximum(c - 1, 0)))

    def next_doc(c):
        return jnp.where(c == chunks - 1, doc_after, first_doc(jnp.minimum(c + 1, chunks - 1)))

    def state_at(k, doc):
        entered = jnp.concatenate([value_of(s_in, 0), value_of(s_in, 1)], axis=1)
        return state[k] + jnp.where(doc == doc_before, phi_f[pl.ds(k, 1), :], 0.0) * entered

    def back_at(k, doc):
        entered = jnp.concatenate([value_of(g_in, 0), value_of(g_in, 1)], axis=1)
        return back[k] + jnp.where(doc == doc_after, phi_b[pl.ds(k, 1), :], 0.0) * entered

    def span_rows(start, count):
        return pl.ds(pl.multiple_of(start, count), count)

    def to_side(near):
        return side - 1 if near else 1

    def r_relay(near):
        start = mod(me_x + side // 2, side) * group + near * (group // 2)
        return pltpu.make_async_remote_copy(
            src_ref=r_acc.at[span_rows(start, group // 2)], dst_ref=r_mid.at[near],
            send_sem=ra_ss.at[near], recv_sem=ra_rs.at[near],
            device_id=at_xy(mod(me_x + to_side(near), side), me_y),
        )

    def r_copy(near):
        x = mod(me_x + to_side(near), side)
        return pltpu.make_async_remote_copy(
            src_ref=r_acc.at[span_rows(x * group, group)], dst_ref=r_in.at[near],
            send_sem=r_ss.at[near], recv_sem=r_rs.at[near], device_id=at_xy(x, me_y),
        )

    def w_relay(near, x):
        start = (x * side + mod(me_y + side // 2, side)) * block + near * (block // 2)
        return pltpu.make_async_remote_copy(
            src_ref=w_acc.at[span_rows(start, block // 2)], dst_ref=w_mid.at[near, x],
            send_sem=wa_ss.at[near, x], recv_sem=wa_rs.at[near, x],
            device_id=at_xy(me_x, mod(me_y + to_side(near), side)),
        )

    def w_copy(near, x):
        y = mod(me_y + to_side(near), side)
        return pltpu.make_async_remote_copy(
            src_ref=w_acc.at[span_rows((x * side + y) * block, block)], dst_ref=w_in.at[near, x],
            send_sem=w_ss.at[near, x], recv_sem=w_rs.at[near, x], device_id=at_xy(me_x, y),
        )

    def r_copy2(o):
        y = mod(me_y + o, side)
        return pltpu.make_async_remote_copy(
            src_ref=r_acc.at[span_rows((me_x * side + y) * block, block)], dst_ref=r_in2.at[o - 1],
            send_sem=r2_ss.at[o - 1], recv_sem=r2_rs.at[o - 1], device_id=at_xy(me_x, y),
        )

    def w_copy2(o):
        x = mod(me_x + o, side)
        return pltpu.make_async_remote_copy(
            src_ref=w_acc.at[span_rows((x * side + me_y) * block, block)], dst_ref=w_in2.at[o - 1],
            send_sem=w2_ss.at[o - 1], recv_sem=w2_rs.at[o - 1], device_id=at_xy(x, me_y),
        )

    def key_grads(c):
        rows = rows_of(c)
        column = doc_col[rows, :]
        half_row = half[pl.ds(c, 1), :]
        before, after = previous_doc(c), next_doc(c)
        sh, sl = two_parts(state_at(c, before) * half_row)
        sphi[c], splo[c] = sh, sl
        bh, bl = two_parts(back_at(c + 1, after) * half_row)
        bphi[c], bplo[c] = bh, bl
        pair = dot_nt(ghi[rows, :], jnp.concatenate([sh, sl], axis=0))
        to_read = pair[:, :states] + pair[:, states:] + dot_nt(glo[rows, :], sh)
        pair = dot_nt(xhi[rows, :], jnp.concatenate([bh, bl], axis=0))
        to_write = pair[:, :states] + pair[:, states:] + dot_nt(xlo[rows, :], bh)
        to_read = jnp.where(column == before, to_read, 0.0)
        to_write = jnp.where(column == after, to_write, 0.0)
        r_acc[rows, :] += to_read
        w_acc[rows, :] += to_write

    both = (0, 1)

    @pl.loop(0, side)
    def _(i):
        o = jnp.where(i == 0, side // 2, jnp.where(i == 1, 1, jnp.where(i == 2, side - 1, 0)))
        x = mod(me_x + o, side)
        pl.loop(0, chunks // side, unroll=True)(lambda k: key_grads(x * (chunks // side) + k))

        @pl.when(i == 0)
        def _():
            for near in both:
                r_relay(near).start()

        for near in both:
            w_relay(near, x).start()

    def per_head(value):
        high, low = two_parts(value)
        return dot_nt(of_head16, high) + dot_nt(of_head16, low)

    def rest(c):
        rows = rows_of(c)
        column = doc_col[rows, :]
        docs = doc_row(c)
        before, after, last = previous_doc(c), next_doc(c), docs[:, q - 1:]
        reads = jnp.where(column == before, r_ref[rows, :].astype(F32), 0.0).astype(BF16)
        writes = jnp.where(column == after, w_ref[rows, :].astype(F32), 0.0).astype(BF16)
        out = out_acc[rows, :] + dot_nn(jnp.concatenate([reads, reads], axis=1), jnp.concatenate([sphi[c], splo[c]], axis=0))
        val = val_acc[rows, :] + dot_nn(jnp.concatenate([writes, writes], axis=1), jnp.concatenate([bphi[c], bplo[c]], axis=0))
        vg_ref[rows, :] = (scale[rows, :] * val).astype(BF16)
        of_chunk = pl.ds(pl.multiple_of(c * heads, heads), heads)
        at_write = shrinks[of_chunk, :] * per_head(x_ref[rows, :].astype(F32) * val)
        at_read = grows[of_chunk, :] * per_head(g_ref[rows, :].astype(F32) * out)
        lower = (jnp.concatenate([column] * doc_rows, axis=1) == docs) & (square_rows >= square_cols)
        later = stacked_dot(at_read - at_write, lower.astype(F32).astype(BF16))
        crossing = jnp.sum(state_at(c + 1, last) * back_at(c + 1, after), axis=0, keepdims=True)
        crossing = jnp.sum(of_head * crossing, axis=1, keepdims=True)
        crossing = jnp.where(last == after, crossing, 0.0)
        later = later + jnp.where(docs == last, crossing, 0.0)
        sg_ref[:, rows] = at_write / step_ref[:, rows] - rate * later

    middle_at, late = (4 * chunks) // 8, (5 * chunks) // 8
    pl.loop(early, middle_at)(within)
    for near in both:
        r_relay(near).wait_recv()
        rows = span_rows(mod(me_x + to_side(near), side) * group + near * (group // 2), group // 2)
        r_acc[rows, :] += r_mid[near]
        r_copy(near).start()
    pl.loop(middle_at, late)(within)

    @pl.loop(0, side)
    def _(x):
        for near in both:
            w_relay(near, x).wait_recv()
            start = (x * side + mod(me_y + to_side(near), side)) * block + near * (block // 2)
            rows = span_rows(start, block // 2)
            w_acc[rows, :] += w_mid[near, x]
            w_copy(near, x).start()

    pl.loop(late, chunks)(within)
    later_from = chunks // 2
    pl.loop(0, later_from, unroll=2)(rest)
    for near in both:
        r_copy(near).wait_recv()

    @pl.loop(0, side)
    def _(x):
        for near in both:
            w_copy(near, x).wait_recv()

    for o in range(side):
        y = mod(me_y + o, side)
        rows = span_rows((me_x * side + y) * block, block)
        held = r_acc[rows, :]
        for k in both:
            held = held + r_in[k, span_rows(y * block, block), :]
        r_acc[rows, :] = held
        if o > 0:
            r_copy2(o).start()
        x = mod(me_x + o, side)
        rows = span_rows((x * side + me_y) * block, block)
        held = w_acc[rows, :]
        for k in both:
            held = held + w_in[k, x]
        w_acc[rows, :] = held
        if o > 0:
            w_copy2(o).start()
    pl.loop(later_from, chunks, unroll=2)(rest)
    mine_rows = span_rows(me * block, block)
    read_total, write_total = r_acc[mine_rows, :], w_acc[mine_rows, :]
    for o in range(1, side):
        r_copy2(o).wait_recv()
        read_total = read_total + r_in2[o - 1]
        w_copy2(o).wait_recv()
        write_total = write_total + w_in2[o - 1]
    kg_ref[0] = -write_total
    kg_ref[1] = -read_total
    for far in (1, 2):
        if far < n_z:

            @pl.when(me_z + far < n_z)
            def _():
                z_copy(0, far).wait_send()

            @pl.when(me_z - far >= 0)
            def _():
                z_copy(1, far).wait_send()

    for near in both:
        r_relay(near).wait_send()
        r_copy(near).wait_send()

    @pl.loop(0, side)
    def _(x):
        for near in both:
            w_relay(near, x).wait_send()
            w_copy(near, x).wait_send()

    for o in range(1, side):
        r_copy2(o).wait_send()
        w_copy2(o).wait_send()


def shards(mesh_shape, values, step_sizes, decay_rates, write_keys, read_keys, doc_ids, out_grad):
    n_ctx, n_head = mesh_shape
    length, width = values.shape
    heads = decay_rates.shape[0]
    states = write_keys.shape[1]
    chunks = length // QCHUNK
    block = length // n_head
    side = math.isqrt(n_head)
    vmem, hbm = pl.BlockSpec(memory_space=pltpu.VMEM), pl.BlockSpec(memory_space=pl.ANY)
    wide16 = pltpu.VMEM((length, width), BF16)
    wide32 = pltpu.VMEM((length, width), F32)
    def messages(count):
        return pltpu.VMEM((count, states + 8, width // 2), F32)

    def semaphores(*shape):
        return [pltpu.SemaphoreType.DMA(shape)] * 2

    others = max(side - 1, 1)
    value_grad, step_grad, key_grad = pl.pallas_call(
        partial(kernel, n_ctx, n_head),
        out_shape=(
            pltpu.VMEM((length, width), BF16),
            pltpu.VMEM((heads, length), F32),
            pltpu.VMEM((2, block, states), F32),
        ),
        in_specs=[hbm, hbm, hbm, pl.BlockSpec(memory_space=pltpu.SMEM), hbm, hbm, hbm],
        out_specs=(vmem, vmem, vmem),
        scratch_shapes=[
            wide16, wide16, pltpu.VMEM((length, states), BF16), pltpu.VMEM((length, states), BF16),
            pltpu.VMEM((heads, length), F32), pltpu.VMEM((length // 128, 128), jnp.int32),
            pltpu.SemaphoreType.DMA((2,)), pltpu.SemaphoreType.DMA((4, chunks)),
            pltpu.VMEM((chunks, 3 * heads, QCHUNK), BF16), pltpu.VMEM((chunks, 3 * heads, QCHUNK), BF16),
            pltpu.VMEM((chunks * heads, QCHUNK), F32), pltpu.VMEM((chunks * heads, QCHUNK), F32),
            pltpu.VMEM((states, width), F32),
            wide16, wide16, wide16, wide16, wide32, wide32, wide32,
            pltpu.VMEM((length, 128), F32),
            pltpu.VMEM((length, states), F32),
            pltpu.VMEM((length, states), F32),
            pltpu.VMEM((2, length // side // 2, states), F32),
            pltpu.VMEM((2, side, block // 2, states), F32),
            pltpu.VMEM((2, length // side, states), F32),
            pltpu.VMEM((2, side, block, states), F32),
            pltpu.VMEM((others, block, states), F32),
            pltpu.VMEM((others, block, states), F32),
            pltpu.VMEM((chunks + 1, states, width), F32),
            pltpu.VMEM((chunks + 1, states, width), F32),
            pltpu.VMEM((chunks, width), F32),
            pltpu.VMEM((chunks + 1, width), F32),
            pltpu.VMEM((chunks + 1, width), F32),
            pltpu.VMEM((chunks, states, width), BF16),
            pltpu.VMEM((chunks, states, width), BF16),
            pltpu.VMEM((chunks, states, width), BF16),
            pltpu.VMEM((chunks, states, width), BF16),
            messages(2), messages(2), messages(1), messages(1), messages(1), messages(1),
            messages(2), messages(2), messages(1), messages(1), messages(2), messages(2),
            *semaphores(2), *semaphores(2, 2), *semaphores(2),
            *semaphores(2), *semaphores(2, side), *semaphores(2), *semaphores(2, side),
            *semaphores(others), *semaphores(others),
        ],
        compiler_params=pltpu.CompilerParams(
            collective_id=0, has_side_effects=True, vmem_limit_bytes=58 * 2**20
        ),
    )(
        values, out_grad, step_sizes.T, decay_rates, write_keys, read_keys,
        doc_ids.reshape(length // 128, 128),
    )
    return value_grad, step_grad.T, -key_grad[0], -key_grad[1]


def solution(mesh):
    return jax.shard_map(
        partial(shards, (mesh.shape["ctx"], mesh.shape["head"])),
        mesh=mesh,
        in_specs=(
            P("ctx", "head"),
            P("ctx", "head"),
            P("head"),
            P("ctx", None),
            P("ctx", None),
            P("ctx"),
            P("ctx", "head"),
        ),
        out_specs=(
            P("ctx", "head"),
            P("ctx", "head"),
            P(("ctx", "head"), None),
            P(("ctx", "head"), None),
        ),
        check_vma=False,
    )
```

```python
import math
from functools import partial

import jax
import jax.numpy as jnp
from jax import lax
from jax.experimental import pallas as pl
from jax.experimental.pallas import tpu as pltpu
from jax.sharding import PartitionSpec as P

QCHUNK = 256
F32 = jnp.float32
BF16 = jnp.bfloat16


def two_parts(value):
    high = value.astype(BF16)
    return high, (value - high.astype(F32)).astype(BF16)


def three_parts(value):
    high = value.astype(BF16)
    rest = value - high.astype(F32)
    middle = rest.astype(BF16)
    return high, middle, (rest - middle.astype(F32)).astype(BF16)


def dot(left, right, contract):
    return lax.dot_general(left, right, ((contract[:1], contract[1:]), ((), ())), preferred_element_type=F32)


def dot_nn(left, right):
    return dot(left, right, (1, 0))


def dot_nt(left, right):
    return dot(left, right, (1, 1))


def dot_tn(left, right):
    return dot(left, right, (0, 0))


def mod(value, count):
    return lax.rem(value + count, count)


def kernel(
    n_ctx, n_head, x_hbm, g_hbm, step_hbm, rate_ref, w_hbm, r_hbm, doc_hbm,
    vg_ref, kg_ref,
    x_ref, g_ref, w_ref, r_ref, step_ref, doc_ref, small_sems, in_sems, u_parts, v_parts, grows, shrinks, entry,
    xhi, xlo, ghi, glo, scale, out_acc, val_acc, doc_col,
    r_acc, w_acc, r_mid, w_mid, r_in, w_in, r_in2, w_in2,
    state, back, half, phi_f, phi_b, sphi, splo, bphi, bplo,
    e_out, b_out, e_sib, b_sib, f_out, k_out, f_in, k_in, s_out, g_out, s_in, g_in,
    sib_ss, sib_rs, z_ss, z_rs, last_ss, last_rs,
    ra_ss, ra_rs, wa_ss, wa_rs, r_ss, r_rs, w_ss, w_rs, r2_ss, r2_rs, w2_ss, w2_rs,
):
    length, width = x_hbm.shape
    heads = step_hbm.shape[0]
    head_size = width // heads
    states = w_hbm.shape[1]
    q = QCHUNK
    chunks = length // q
    side = math.isqrt(n_head)
    n_z = n_ctx // 2
    group = length // side
    block = length // n_head
    lanes = 128
    doc_rows = q // lanes
    hw = width // 2
    me_ctx, me = lax.axis_index("ctx"), lax.axis_index("head")
    me_z, core = me_ctx // 2, lax.rem(me_ctx, 2)
    me_x, me_y = me // side, lax.rem(me, side)

    def at_z(z):
        return {"ctx": z * 2 + core}

    def at_xy(x, y):
        return {"head": x * side + y}

    sibling = {"ctx": me_ctx + 1 - 2 * core}

    def put(ref, which, value, span, doc):
        ref[which, 0:states, :] = value
        ref[which, states:states + 1, :] = span
        ref[which, states + 1:states + 2, :] = jnp.broadcast_to(doc, (1, hw))

    def arrivals(c):
        rows = pl.ds(pl.multiple_of(c * q, q), q)
        pairs = ((g_hbm, g_ref), (x_hbm, x_ref), (w_hbm, w_ref), (r_hbm, r_ref))
        return [
            pltpu.make_async_copy(src.at[rows], dst.at[rows], in_sems.at[k, c])
            for k, (src, dst) in enumerate(pairs)
        ]

    small = (
        pltpu.make_async_copy(step_hbm, step_ref, small_sems.at[0]),
        pltpu.make_async_copy(doc_hbm, doc_ref, small_sems.at[1]),
    )
    for copy in small:
        copy.start()

    @pl.loop(0, chunks)
    def _(c):
        for copy in arrivals(c):
            copy.start()

    for far in range(2):
        for ref in (f_in, k_in):
            put(ref, far, jnp.zeros((states, hw), F32), jnp.zeros((1, hw), F32), jnp.full((1, 1), -1.0, F32))

    barrier = pltpu.get_barrier_semaphore()
    pl.semaphore_signal(barrier, inc=1, device_id=sibling)
    for o in range(1, n_z):
        pl.semaphore_signal(barrier, inc=1, device_id=at_z(mod(me_z + o, n_z)))
    for o in range(1, side):
        pl.semaphore_signal(barrier, inc=1, device_id=at_xy(mod(me_x + o, side), me_y))
        pl.semaphore_signal(barrier, inc=1, device_id=at_xy(me_x, mod(me_y + o, side)))

    head_rows = lax.broadcasted_iota(jnp.int32, (heads, width), 0)
    head_lanes = lax.broadcasted_iota(jnp.int32, (heads, width), 1)
    of_head = jnp.where(head_lanes // head_size == head_rows, 1.0, 0.0)
    of_head16 = of_head.astype(BF16)
    spread3 = jnp.concatenate([of_head] * 3, axis=0).astype(BF16)
    square_rows = lax.broadcasted_iota(jnp.int32, (q, q), 0)
    square_cols = lax.broadcasted_iota(jnp.int32, (q, q), 1)
    rate = jnp.zeros((heads, 1), F32)
    rate_row = lax.broadcasted_iota(jnp.int32, (heads, 1), 0)
    for h in range(heads):
        rate = jnp.where(rate_row == h, rate_ref[h], rate)

    def rows_of(c):
        return pl.ds(pl.multiple_of(c * q, q), q)

    def doc_row(c):
        return jnp.concatenate(
            [doc_ref[pl.ds(c * doc_rows + k, 1), :] for k in range(doc_rows)], axis=1
        ).astype(F32)

    def first_doc(c):
        return doc_ref[pl.ds(c * doc_rows, 1), 0:1].astype(F32)

    def last_doc(c):
        return doc_ref[pl.ds(c * doc_rows + doc_rows - 1, 1), lanes - 1:lanes].astype(F32)

    def to_lanes(column):
        return jnp.sum(of_head * column, axis=0, keepdims=True)

    def stacked_parts(value):
        return jnp.concatenate([p.astype(F32) for p in three_parts(value)], axis=0).astype(BF16)

    def stacked_dot(value, right):
        made = dot_nn(stacked_parts(value), right)
        count = value.shape[0]
        return made[:count] + made[count:2 * count] + made[2 * count:]

    for copy in small:
        copy.wait()
    all_steps = jnp.concatenate([step_ref[:, c * q:(c + 1) * q] for c in range(chunks)], axis=0)
    all_rates = jnp.concatenate([rate] * chunks, axis=0)
    decay = stacked_dot(-all_steps * all_rates, (square_rows <= square_cols).astype(F32).astype(BF16))
    whole = decay[:, q - 1:q]
    from_middle = decay - 0.5 * whole
    grow, shrink = jnp.exp(from_middle), jnp.exp(-from_middle) * all_steps
    grows[...], shrinks[...] = grow, shrink
    total = jnp.zeros((heads, 1), F32)
    for c in range(chunks):
        of_chunk = slice(c * heads, (c + 1) * heads)
        u_parts[c] = stacked_parts(grow[of_chunk])
        v_parts[c] = stacked_parts(shrink[of_chunk])
        half[c:c + 1, :] = to_lanes(jnp.exp(0.5 * whole[of_chunk]))
        phi_f[c:c + 1, :] = to_lanes(jnp.exp(total))
        total = total + whole[of_chunk]

    state[0] = jnp.zeros((states, width), F32)
    back[chunks] = jnp.zeros((states, width), F32)

    def local_states(c):
        rows = rows_of(c)
        for copy in arrivals(c):
            copy.wait()
        high, low = two_parts(g_ref[rows, :].astype(F32) * dot_tn(u_parts[c], spread3))
        ghi[rows, :], glo[rows, :] = high, low
        x_scale = dot_tn(v_parts[c], spread3)
        scale[rows, :] = x_scale
        xh, xl = two_parts(x_ref[rows, :].astype(F32) * x_scale)
        xhi[rows, :], xlo[rows, :] = xh, xl
        docs = doc_row(c)
        column = jnp.transpose(jnp.broadcast_to(docs, (lanes, q)))
        doc_col[rows, :] = column
        half_row = half[pl.ds(c, 1), :]
        w_last = jnp.where(column == docs[:, q - 1:], w_ref[rows, :].astype(F32), 0.0).astype(BF16)
        r_first = jnp.where(column == docs[:, :1], r_ref[rows, :].astype(F32), 0.0).astype(BF16)
        made = (dot_tn(w_last, xh) + dot_tn(w_last, xl)) * half_row
        before = last_doc(jnp.maximum(c - 1, 0))
        kept = jnp.where(before == docs[:, q - 1:], half_row * half_row, 0.0)
        state[c + 1] = made + kept * state[c]
        made = (dot_tn(r_first, high) + dot_tn(r_first, low)) * half_row
        back[c] = made
        reached = jnp.where(docs[:, :1] == first_doc(0), phi_f[pl.ds(c, 1), :], 0.0)
        entry[...] = jnp.where(c == 0, made, entry[...] + reached * made)

    pl.loop(0, chunks, unroll=2)(local_states)
    phi_f[pl.ds(chunks, 1), :] = to_lanes(jnp.exp(total))
    whole_row = to_lanes(total)
    first_here, last_here = first_doc(0), last_doc(chunks - 1)

    def span_of(ref, which):
        return ref[which, states:states + 1, :]

    def doc_of(ref, which):
        return ref[which, states + 1:states + 2, :]

    def value_of(ref, which):
        return ref[which, 0:states, :]

    def joined(near, near_doc, near_span, far, far_doc):
        return near + jnp.where(near_doc == far_doc, jnp.exp(near_span), 0.0) * far

    def sib_copy(k, src, dst, ss, rs):
        return pltpu.make_async_remote_copy(
            src_ref=src, dst_ref=dst, send_sem=ss.at[k], recv_sem=rs.at[k], device_id=sibling
        )

    def z_copy(k, far):
        src, dst, to = (f_out, f_in, me_z + far) if k == 0 else (k_out, k_in, me_z - far)
        return pltpu.make_async_remote_copy(
            src_ref=src.at[0], dst_ref=dst.at[far - 1], send_sem=z_ss.at[k, far - 1],
            recv_sem=z_rs.at[k, far - 1], device_id=at_z(to),
        )

    def same_doc(c, rows):
        return jnp.concatenate([doc_col[rows, :]] * doc_rows, axis=1) == doc_row(c)

    def pairs(c):
        rows = rows_of(c)
        reads, writes = r_ref[rows, :], w_ref[rows, :]
        lower = same_doc(c, rows) & (square_rows >= square_cols)
        xh, xl, gh, gl = xhi[rows, :], xlo[rows, :], ghi[rows, :], glo[rows, :]
        made = dot_nt(gh, xh) + dot_nt(gh, xl) + dot_nt(gl, xh)
        high, low = two_parts(jnp.where(lower, made, 0.0))
        r_acc[rows, :] = dot_nn(high, writes) + dot_nn(low, writes)
        w_acc[rows, :] = jnp.transpose(dot_tn(reads, high) + dot_tn(reads, low))

    def within(c):
        rows = rows_of(c)
        reads, writes = r_ref[rows, :], w_ref[rows, :]
        same = same_doc(c, rows)
        lower = same & (square_rows >= square_cols)
        upper = same & (square_rows <= square_cols)
        xh, xl, gh, gl = xhi[rows, :], xlo[rows, :], ghi[rows, :], glo[rows, :]
        high, low = two_parts(jnp.where(lower, dot_nt(reads, writes), 0.0))
        out_acc[rows, :] = dot_nn(high, xh) + dot_nn(high, xl) + dot_nn(low, xh)
        high, low = two_parts(jnp.where(upper, dot_nt(writes, reads), 0.0))
        val_acc[rows, :] = dot_nn(high, gh) + dot_nn(high, gl) + dot_nn(low, gh)

    for k in range(2):
        lane = slice(k * hw, (k + 1) * hw)
        put(e_out, k, state[chunks][:, lane], whole_row[:, lane], last_here)
        put(b_out, k, entry[:, lane], whole_row[:, lane], first_here)
    pl.semaphore_wait(barrier, 1 + n_z - 1 + 2 * (side - 1))
    sib_copies = (
        sib_copy(0, e_out.at[1 - core], e_sib.at[0], sib_ss, sib_rs),
        sib_copy(1, b_out.at[1 - core], b_sib.at[0], sib_ss, sib_rs),
    )
    for copy in sib_copies:
        copy.start()
    phi_b[pl.ds(chunks, 1), :] = jnp.ones((1, width), F32)

    @pl.loop(0, chunks)
    def _(i):
        c = chunks - 1 - i
        half_row = half[pl.ds(c, 1), :]
        square = half_row * half_row
        kept = jnp.where(first_doc(jnp.minimum(c + 1, chunks - 1)) == first_doc(c), square, 0.0)
        back[c] = back[c] + kept * back[c + 1]
        phi_b[pl.ds(c, 1), :] = phi_b[pl.ds(c + 1, 1), :] * square

    first, early = chunks // 8, (3 * chunks) // 8
    for copy in sib_copies:
        copy.wait()
    low, mine, other = core == 0, core, 0
    e_low = jnp.where(low, value_of(e_out, mine), value_of(e_sib, other))
    e_high = jnp.where(low, value_of(e_sib, other), value_of(e_out, mine))
    b_low = jnp.where(low, value_of(b_out, mine), value_of(b_sib, other))
    b_high = jnp.where(low, value_of(b_sib, other), value_of(b_out, mine))
    span_low = jnp.where(low, span_of(e_out, mine), span_of(e_sib, other))
    span_high = jnp.where(low, span_of(e_sib, other), span_of(e_out, mine))
    last_low = jnp.where(low, doc_of(e_out, mine), doc_of(e_sib, other))
    last_high = jnp.where(low, doc_of(e_sib, other), doc_of(e_out, mine))
    first_low = jnp.where(low, doc_of(b_out, mine), doc_of(b_sib, other))
    first_high = jnp.where(low, doc_of(b_sib, other), doc_of(b_out, mine))
    put(f_out, 0, joined(e_high, last_high, span_high, e_low, last_low), span_low + span_high, last_high)
    put(k_out, 0, joined(b_low, first_low, span_low, b_high, first_high), span_low + span_high, first_low)
    for far in (1, 2):
        if far < n_z:

            @pl.when(me_z + far < n_z)
            def _():
                z_copy(0, far).start()

            @pl.when(me_z - far >= 0)
            def _():
                z_copy(1, far).start()

    pl.loop(0, chunks)(pairs)
    pl.loop(first, early)(within)
    for far in (1, 2):
        if far < n_z:

            @pl.when(me_z - far >= 0)
            def _():
                z_copy(0, far).wait_recv()

            @pl.when(me_z + far < n_z)
            def _():
                z_copy(1, far).wait_recv()

    s_chip = joined(value_of(f_in, 0), doc_of(f_in, 0), span_of(f_in, 0), value_of(f_in, 1), doc_of(f_in, 1))
    g_chip = joined(value_of(k_in, 0), doc_of(k_in, 0), span_of(k_in, 0), value_of(k_in, 1), doc_of(k_in, 1))
    s_high = joined(value_of(e_out, mine), last_low, span_low, s_chip, doc_of(f_in, 0))
    s_high = jnp.where(low, s_high, joined(value_of(e_sib, other), last_low, span_low, s_chip, doc_of(f_in, 0)))
    g_low = joined(value_of(b_sib, other), first_high, span_high, g_chip, doc_of(k_in, 0))
    g_low = jnp.where(low, g_low, joined(value_of(b_out, mine), first_high, span_high, g_chip, doc_of(k_in, 0)))
    s_doc_low, s_doc_high = doc_of(f_in, 0), last_low
    g_doc_low, g_doc_high = first_high, doc_of(k_in, 0)
    put(s_out, 0, jnp.where(low, s_high, s_chip), span_low, jnp.where(low, s_doc_high, s_doc_low))
    put(g_out, 0, jnp.where(low, g_chip, g_low), span_low, jnp.where(low, g_doc_high, g_doc_low))
    last_copies = (
        sib_copy(0, s_out.at[0], s_in.at[mine], last_ss, last_rs),
        sib_copy(1, g_out.at[0], g_in.at[mine], last_ss, last_rs),
    )
    for copy in last_copies:
        copy.start()
    put(s_in, mine, jnp.where(low, s_chip, s_high), span_low, jnp.where(low, s_doc_low, s_doc_high))
    put(g_in, mine, jnp.where(low, g_low, g_chip), span_low, jnp.where(low, g_doc_low, g_doc_high))
    pl.loop(0, first)(within)
    for copy in last_copies:
        copy.wait()

    doc_before, doc_after = doc_of(s_in, 0)[:, :1], doc_of(g_in, 0)[:, :1]

    def previous_doc(c):
        return jnp.where(c == 0, doc_before, last_doc(jnp.maximum(c - 1, 0)))

    def next_doc(c):
        return jnp.where(c == chunks - 1, doc_after, first_doc(jnp.minimum(c + 1, chunks - 1)))

    def state_at(k, doc):
        entered = jnp.concatenate([value_of(s_in, 0), value_of(s_in, 1)], axis=1)
        return state[k] + jnp.where(doc == doc_before, phi_f[pl.ds(k, 1), :], 0.0) * entered

    def back_at(k, doc):
        entered = jnp.concatenate([value_of(g_in, 0), value_of(g_in, 1)], axis=1)
        return back[k] + jnp.where(doc == doc_after, phi_b[pl.ds(k, 1), :], 0.0) * entered

    def span_rows(start, count):
        return pl.ds(pl.multiple_of(start, count), count)

    def to_side(near):
        return side - 1 if near else 1

    def r_relay(near):
        start = mod(me_x + side // 2, side) * group + near * (group // 2)
        return pltpu.make_async_remote_copy(
            src_ref=r_acc.at[span_rows(start, group // 2)], dst_ref=r_mid.at[near],
            send_sem=ra_ss.at[near], recv_sem=ra_rs.at[near],
            device_id=at_xy(mod(me_x + to_side(near), side), me_y),
        )

    def r_copy(near):
        x = mod(me_x + to_side(near), side)
        return pltpu.make_async_remote_copy(
            src_ref=r_acc.at[span_rows(x * group, group)], dst_ref=r_in.at[near],
            send_sem=r_ss.at[near], recv_sem=r_rs.at[near], device_id=at_xy(x, me_y),
        )

    def w_relay(near, x):
        start = (x * side + mod(me_y + side // 2, side)) * block + near * (block // 2)
        return pltpu.make_async_remote_copy(
            src_ref=w_acc.at[span_rows(start, block // 2)], dst_ref=w_mid.at[near, x],
            send_sem=wa_ss.at[near, x], recv_sem=wa_rs.at[near, x],
            device_id=at_xy(me_x, mod(me_y + to_side(near), side)),
        )

    def w_copy(near, x):
        y = mod(me_y + to_side(near), side)
        return pltpu.make_async_remote_copy(
            src_ref=w_acc.at[span_rows((x * side + y) * block, block)], dst_ref=w_in.at[near, x],
            send_sem=w_ss.at[near, x], recv_sem=w_rs.at[near, x], device_id=at_xy(me_x, y),
        )

    def r_copy2(o):
        y = mod(me_y + o, side)
        return pltpu.make_async_remote_copy(
            src_ref=r_acc.at[span_rows((me_x * side + y) * block, block)], dst_ref=r_in2.at[o - 1],
            send_sem=r2_ss.at[o - 1], recv_sem=r2_rs.at[o - 1], device_id=at_xy(me_x, y),
        )

    def w_copy2(o):
        x = mod(me_x + o, side)
        return pltpu.make_async_remote_copy(
            src_ref=w_acc.at[span_rows((x * side + me_y) * block, block)], dst_ref=w_in2.at[o - 1],
            send_sem=w2_ss.at[o - 1], recv_sem=w2_rs.at[o - 1], device_id=at_xy(x, me_y),
        )

    def key_grads(c):
        rows = rows_of(c)
        column = doc_col[rows, :]
        half_row = half[pl.ds(c, 1), :]
        before, after = previous_doc(c), next_doc(c)
        sh, sl = two_parts(state_at(c, before) * half_row)
        sphi[c], splo[c] = sh, sl
        bh, bl = two_parts(back_at(c + 1, after) * half_row)
        bphi[c], bplo[c] = bh, bl
        pair = dot_nt(ghi[rows, :], jnp.concatenate([sh, sl], axis=0))
        to_read = pair[:, :states] + pair[:, states:] + dot_nt(glo[rows, :], sh)
        pair = dot_nt(xhi[rows, :], jnp.concatenate([bh, bl], axis=0))
        to_write = pair[:, :states] + pair[:, states:] + dot_nt(xlo[rows, :], bh)
        to_read = jnp.where(column == before, to_read, 0.0)
        to_write = jnp.where(column == after, to_write, 0.0)
        r_acc[rows, :] += to_read
        w_acc[rows, :] += to_write

    both = (0, 1)

    @pl.loop(0, side)
    def _(i):
        o = jnp.where(i == 0, side // 2, jnp.where(i == 1, 1, jnp.where(i == 2, side - 1, 0)))
        x = mod(me_x + o, side)
        pl.loop(0, chunks // side, unroll=True)(lambda k: key_grads(x * (chunks // side) + k))

        @pl.when(i == 0)
        def _():
            for near in both:
                r_relay(near).start()

        for near in both:
            w_relay(near, x).start()

    def per_head(value):
        high, low = two_parts(value)
        return dot_nt(of_head16, high) + dot_nt(of_head16, low)

    def rest(c):
        rows = rows_of(c)
        column = doc_col[rows, :]
        docs = doc_row(c)
        before, after, last = previous_doc(c), next_doc(c), docs[:, q - 1:]
        reads = jnp.where(column == before, r_ref[rows, :].astype(F32), 0.0).astype(BF16)
        writes = jnp.where(column == after, w_ref[rows, :].astype(F32), 0.0).astype(BF16)
        out = out_acc[rows, :] + dot_nn(jnp.concatenate([reads, reads], axis=1), jnp.concatenate([sphi[c], splo[c]], axis=0))
        val = val_acc[rows, :] + dot_nn(jnp.concatenate([writes, writes], axis=1), jnp.concatenate([bphi[c], bplo[c]], axis=0))
        vg_ref[rows, :] = (scale[rows, :] * val).astype(BF16)
        of_chunk = pl.ds(pl.multiple_of(c * heads, heads), heads)
        at_write = shrinks[of_chunk, :] * per_head(x_ref[rows, :].astype(F32) * val)
        at_read = grows[of_chunk, :] * per_head(g_ref[rows, :].astype(F32) * out)
        lower = (jnp.concatenate([column] * doc_rows, axis=1) == docs) & (square_rows >= square_cols)
        later = stacked_dot(at_read - at_write, lower.astype(F32).astype(BF16))
        crossing = jnp.sum(state_at(c + 1, last) * back_at(c + 1, after), axis=0, keepdims=True)
        crossing = jnp.sum(of_head * crossing, axis=1, keepdims=True)
        crossing = jnp.where(last == after, crossing, 0.0)
        later = later + jnp.where(docs == last, crossing, 0.0)
        step_grad = rate * later - at_write / step_ref[:, rows]
        for k in range(doc_rows):
            at = pl.ds(pl.multiple_of((c * doc_rows + k) * heads, heads), heads)
            kg_ref[2, at, :] = step_grad[:, k * lanes:(k + 1) * lanes]

    middle_at, late = (4 * chunks) // 8, (5 * chunks) // 8
    pl.loop(early, middle_at)(within)
    for near in both:
        r_relay(near).wait_recv()
        rows = span_rows(mod(me_x + to_side(near), side) * group + near * (group // 2), group // 2)
        r_acc[rows, :] += r_mid[near]
        r_copy(near).start()
    pl.loop(middle_at, late)(within)

    @pl.loop(0, side)
    def _(x):
        for near in both:
            w_relay(near, x).wait_recv()
            start = (x * side + mod(me_y + to_side(near), side)) * block + near * (block // 2)
            rows = span_rows(start, block // 2)
            w_acc[rows, :] += w_mid[near, x]
            w_copy(near, x).start()

    pl.loop(late, chunks)(within)
    later_from = chunks // 2
    pl.loop(0, later_from, unroll=2)(rest)
    for near in both:
        r_copy(near).wait_recv()

    @pl.loop(0, side)
    def _(x):
        for near in both:
            w_copy(near, x).wait_recv()

    for o in range(side):
        y = mod(me_y + o, side)
        rows = span_rows((me_x * side + y) * block, block)
        held = r_acc[rows, :]
        for k in both:
            held = held + r_in[k, span_rows(y * block, block), :]
        r_acc[rows, :] = held
        if o > 0:
            r_copy2(o).start()
        x = mod(me_x + o, side)
        rows = span_rows((x * side + me_y) * block, block)
        held = w_acc[rows, :]
        for k in both:
            held = held + w_in[k, x]
        w_acc[rows, :] = held
        if o > 0:
            w_copy2(o).start()
    pl.loop(later_from, chunks, unroll=2)(rest)
    mine_rows = span_rows(me * block, block)
    read_total, write_total = r_acc[mine_rows, :], w_acc[mine_rows, :]
    for o in range(1, side):
        r_copy2(o).wait_recv()
        read_total = read_total + r_in2[o - 1]
        w_copy2(o).wait_recv()
        write_total = write_total + w_in2[o - 1]
    kg_ref[0] = -write_total
    kg_ref[1] = -read_total
    for far in (1, 2):
        if far < n_z:

            @pl.when(me_z + far < n_z)
            def _():
                z_copy(0, far).wait_send()

            @pl.when(me_z - far >= 0)
            def _():
                z_copy(1, far).wait_send()

    for near in both:
        r_relay(near).wait_send()
        r_copy(near).wait_send()

    @pl.loop(0, side)
    def _(x):
        for near in both:
            w_relay(near, x).wait_send()
            w_copy(near, x).wait_send()

    for o in range(1, side):
        r_copy2(o).wait_send()
        w_copy2(o).wait_send()


def shards(mesh_shape, values, step_sizes, decay_rates, write_keys, read_keys, doc_ids, out_grad):
    n_ctx, n_head = mesh_shape
    length, width = values.shape
    heads = decay_rates.shape[0]
    states = write_keys.shape[1]
    chunks = length // QCHUNK
    block = length // n_head
    side = math.isqrt(n_head)
    vmem, hbm = pl.BlockSpec(memory_space=pltpu.VMEM), pl.BlockSpec(memory_space=pl.ANY)
    wide16 = pltpu.VMEM((length, width), BF16)
    wide32 = pltpu.VMEM((length, width), F32)
    def messages(count):
        return pltpu.VMEM((count, states + 8, width // 2), F32)

    def semaphores(*shape):
        return [pltpu.SemaphoreType.DMA(shape)] * 2

    others = max(side - 1, 1)
    value_grad, small_grads = pl.pallas_call(
        partial(kernel, n_ctx, n_head),
        out_shape=(
            pltpu.VMEM((length, width), BF16),
            pltpu.VMEM((3, block, states), F32),
        ),
        in_specs=[hbm, hbm, hbm, pl.BlockSpec(memory_space=pltpu.SMEM), hbm, hbm, hbm],
        out_specs=(vmem, vmem),
        scratch_shapes=[
            wide16, wide16, pltpu.VMEM((length, states), BF16), pltpu.VMEM((length, states), BF16),
            pltpu.VMEM((heads, length), F32), pltpu.VMEM((length // 128, 128), jnp.int32),
            pltpu.SemaphoreType.DMA((2,)), pltpu.SemaphoreType.DMA((4, chunks)),
            pltpu.VMEM((chunks, 3 * heads, QCHUNK), BF16), pltpu.VMEM((chunks, 3 * heads, QCHUNK), BF16),
            pltpu.VMEM((chunks * heads, QCHUNK), F32), pltpu.VMEM((chunks * heads, QCHUNK), F32),
            pltpu.VMEM((states, width), F32),
            wide16, wide16, wide16, wide16, wide32, wide32, wide32,
            pltpu.VMEM((length, 128), F32),
            pltpu.VMEM((length, states), F32),
            pltpu.VMEM((length, states), F32),
            pltpu.VMEM((2, length // side // 2, states), F32),
            pltpu.VMEM((2, side, block // 2, states), F32),
            pltpu.VMEM((2, length // side, states), F32),
            pltpu.VMEM((2, side, block, states), F32),
            pltpu.VMEM((others, block, states), F32),
            pltpu.VMEM((others, block, states), F32),
            pltpu.VMEM((chunks + 1, states, width), F32),
            pltpu.VMEM((chunks + 1, states, width), F32),
            pltpu.VMEM((chunks, width), F32),
            pltpu.VMEM((chunks + 1, width), F32),
            pltpu.VMEM((chunks + 1, width), F32),
            pltpu.VMEM((chunks, states, width), BF16),
            pltpu.VMEM((chunks, states, width), BF16),
            pltpu.VMEM((chunks, states, width), BF16),
            pltpu.VMEM((chunks, states, width), BF16),
            messages(2), messages(2), messages(1), messages(1), messages(1), messages(1),
            messages(2), messages(2), messages(1), messages(1), messages(2), messages(2),
            *semaphores(2), *semaphores(2, 2), *semaphores(2),
            *semaphores(2), *semaphores(2, side), *semaphores(2), *semaphores(2, side),
            *semaphores(others), *semaphores(others),
        ],
        compiler_params=pltpu.CompilerParams(
            collective_id=0, has_side_effects=True, vmem_limit_bytes=58 * 2**20
        ),
    )(
        values, out_grad, step_sizes.T, decay_rates, write_keys, read_keys,
        doc_ids.reshape(length // 128, 128),
    )
    step_grad = (-small_grads[2]).reshape(length // 128, heads, 128).transpose(0, 2, 1).reshape(length, heads)
    return value_grad, step_grad, -small_grads[0], -small_grads[1]


def solution(mesh):
    return jax.shard_map(
        partial(shards, (mesh.shape["ctx"], mesh.shape["head"])),
        mesh=mesh,
        in_specs=(
            P("ctx", "head"),
            P("ctx", "head"),
            P("head"),
            P("ctx", None),
            P("ctx", None),
            P("ctx"),
            P("ctx", "head"),
        ),
        out_specs=(
            P("ctx", "head"),
            P("ctx", "head"),
            P(("ctx", "head"), None),
            P(("ctx", "head"), None),
        ),
        check_vma=False,
    )
```
